32 devices in a mesh: pipe: 4 (over y, x), dp: 8 (over z, core).
Axes of the slice: x: 2, y: 2, z: 4, core: 2. Of those that a mesh axis runs over, the one named last changes fastest.
Arguments:
- activations: bfloat16 [2, 4, 1024, 6144], P(None, 'pipe', 'dp'), may hold values from -6 to 6
- queries: bfloat16 [2, 4, 1024, 128], P(None, 'pipe', 'dp'), may hold values from -16 to 16
- keys: bfloat16 [2, 4, 1024, 128], P(None, 'pipe', 'dp'), may hold values from -16 to 16
- grad_out: bfloat16 [2, 4, 1024, 128], P(None, 'pipe', 'dp'), may hold values from -0.4375 to 0.4375
- segment_ids: int32 [2, 4, 8, 128], P(None, 'pipe', 'dp'), may hold values from 0 to 3, never falling along the last dimension, each value on 1 to 64 neighbouring positions
Outputs:
- grad_value: bfloat16 [4, 6144, 128], P('pipe', 'dp')
The draws below stay inside these ranges and needn't reach their ends.
Inputs may be any that keep to these rules, and one draw needn't show every extreme that they name: `segment_ids`: ids restart at 0 in every micro-batch; each document spans 1 to 64 tokens, one exactly that many.
All inputs are finite; a program needn't handle non-finite values.
Results may differ from the reference program's by a relative error of at most 0.0063.
Values sent between devices are 32-bit elements; how exact they have to be, the bound alone decides.
No kernel may reach another device: no remote copies, remote signals or barrier semaphores. Data moves between devices by JAX's collectives and lax.ppermute only.
A program may use at most 64 MiB of HBM per device.

```python
import math
import jax
import jax.numpy as jnp
import numpy as np
from jax import lax

D = 6144
HEAD = 128
MB_LEN = 128
DOCS = 4
SECTIONS = 4
TOKENS = 1024
N_DP = 8


def query_key_pair(key):
    base_key = jax.random.fold_in(key, 4242)
    query_key, key_key = jax.random.split(base_key, 2)
    shape = (2, SECTIONS, TOKENS, HEAD)
    query_draw = jnp.clip(jax.random.normal(query_key, shape, jnp.float32), -6.0, 6.0)
    key_draw = jnp.clip(jax.random.normal(key_key, shape, jnp.float32), -6.0, 6.0)
    return (query_draw, key_draw)


def draw_queries(key, part):
    return query_key_pair(key)[0].astype(jnp.bfloat16)


def draw_keys(key, part):
    return query_key_pair(key)[1].astype(jnp.bfloat16)


def with_spikes(result, stream_key, source, target, blocks, factor):
    def block_of(dim):
        return (jnp.arange(result.shape[dim]) // (result.shape[dim] // blocks)).reshape((-1,) + (1,) * (result.ndim - 1 - dim))

    one_side = jax.random.permutation(stream_key, blocks)[block_of(target)]
    second = (block_of(target) + blocks // 2) % blocks
    return jnp.where((block_of(source) == one_side) | (block_of(source) == second), factor * result, result)


def block_scale(stream_key, dims, shards, least, top_value):
    gain, own = 1.0, jax.random.fold_in(stream_key, 6)
    for dim, shards_of in shards:
        steps = jnp.exp(jax.random.uniform(jax.random.fold_in(own, dim), (shards_of,), jnp.float32, least / len(shards), top_value / len(shards)))
        gain = gain * jnp.repeat(steps, dims[dim] // shards_of).reshape([-1 if axis == dim else 1 for axis in range(len(dims))])
    return gain


def profile(number_of, total, bound, slope):
    weights = [(1 << 20) // math.isqrt(standing ** slope) + 1 for standing in range(2, number_of + 1)]
    spare, counts = total - bound - (number_of - 1), [1] * (number_of - 1)
    while spare > 0:
        candidates = [i for i in range(number_of - 1) if counts[i] < bound]
        pool, left = sum([weights[i] for i in candidates]), spare
        for i in candidates:
            addition = min(bound - counts[i], max(1, left * weights[i] // pool), spare)
            counts[i] = counts[i] + addition
            spare = spare - addition
    return np.array([bound] + counts)


def ragged_sizes(stream_key, count, total, bound, skew):
    if count == 2:
        one = jax.random.randint(stream_key, (), max(1, total - bound), min(bound, total - 1) + 1)
        return jnp.stack([one, total - one])
    tallies = jnp.asarray(profile(count, total, bound, skew), jnp.int32)
    couples = (count - 1) // 2
    giver, taker = tallies[1:1 + 2 * couples:2], tallies[2:2 + 2 * couples:2]
    room = jnp.minimum(giver - 1, bound - taker)
    moved = jax.random.randint(jax.random.fold_in(stream_key, 1), (couples,), 0, 1 << 20) % (room + 1)
    tallies = tallies.at[1:1 + 2 * couples:2].set(giver - moved).at[2:2 + 2 * couples:2].set(taker + moved)
    return tallies[jax.random.permutation(jax.random.fold_in(stream_key, 2), count)]


def normal_values(key, extent, deviation, bound, cuts=(), held_as=jnp.bfloat16):
    factor_of = block_scale(key, extent, cuts, -0.22, 0.18) if cuts else 1.0
    result = jax.random.normal(key, extent, jnp.float32) * deviation * factor_of
    return jnp.minimum(jnp.maximum(result, -bound), bound).astype(held_as)


def heavy_noise(own_key, dims, width, bound, pieces, heavy, kind=jnp.bfloat16):
    values = width * jax.random.normal(own_key, dims, jnp.float32)
    if pieces:
        values = values * block_scale(own_key, dims, pieces, -0.22, 0.18)
    return jnp.clip(with_spikes(values, jax.random.fold_in(own_key, 3), *heavy), -bound, bound).astype(kind)


def setup_inputs(seed: int = 0) -> dict:
    splits = jax.random.split(jax.random.key(seed), 6)
    activations = heavy_noise(splits[0], (2, SECTIONS, TOKENS, D), 1.0, 6.0, ((1, 4), (2, 8)), (2, 3, 8, 2.0))
    queries = draw_queries(jax.random.fold_in(splits[5], 71), 0)
    keys = draw_keys(jax.random.fold_in(splits[5], 71), 0)
    grad_out = normal_values(splits[3], (2, SECTIONS, TOKENS, HEAD), 0.03, 0.4375, ((1, 4), (2, 8)))
    segment_ids = jax.vmap(lambda own: jnp.searchsorted(jnp.cumsum(ragged_sizes(own, DOCS, MB_LEN, MB_LEN // 2, 2)), jnp.arange(MB_LEN), side="right"))(jax.random.split(splits[4], 2 * SECTIONS * N_DP)).reshape((2, SECTIONS, N_DP, MB_LEN)).astype(jnp.int32)
    return {"activations": activations, "queries": queries, "keys": keys, "grad_out": grad_out, "segment_ids": segment_ids}


def replica_partial(acts, query_rows, key_rows, grad_rows, segs):
    scores = jnp.dot(query_rows, key_rows.T, preferred_element_type=jnp.float32) / jnp.sqrt(jnp.float32(HEAD))
    position = jnp.arange(MB_LEN, dtype=jnp.int32)
    keep = (position[None, :] <= position[:, None]) & (segs[None, :] == segs[:, None])
    masked = jnp.where(keep, scores, jnp.float32(-1e+30))
    top = lax.optimization_barrier(jnp.max(masked, axis=1, keepdims=True))
    weights = jnp.where(keep, jnp.exp(masked - top), jnp.float32(0.0))
    probs = (weights / lax.optimization_barrier(jnp.sum(weights, axis=1, keepdims=True))).astype(jnp.bfloat16)
    probs = lax.optimization_barrier(probs)
    grad_v = jnp.einsum('qk,qd->kd', probs.astype(jnp.float32), grad_rows.astype(jnp.float32)).astype(jnp.bfloat16)
    grad_v = lax.optimization_barrier(grad_v)
    partial_value = jnp.einsum('td,te->de', acts.astype(jnp.float32), grad_v.astype(jnp.float32)).astype(jnp.bfloat16)
    return lax.optimization_barrier(partial_value)

def slot_sum(items):
    acts, query_rows, key_rows, grad_rows, segs = items
    parts = jax.vmap(replica_partial)(acts.reshape(N_DP, MB_LEN, D), query_rows.reshape(N_DP, MB_LEN, HEAD), key_rows.reshape(N_DP, MB_LEN, HEAD), grad_rows.reshape(N_DP, MB_LEN, HEAD), segs)
    return lax.optimization_barrier(jnp.sum(parts.astype(jnp.float32), axis=0))

def reference(activations, queries, keys, grad_out, segment_ids):
    count = 2 * SECTIONS
    sums = lax.map(slot_sum, (activations.reshape(count, TOKENS, D), queries.reshape(count, TOKENS, HEAD), keys.reshape(count, TOKENS, HEAD), grad_out.reshape(count, TOKENS, HEAD), segment_ids.reshape(count, N_DP, MB_LEN)))
    sums = sums.reshape(2, SECTIONS, D, HEAD)
    total = sums[0] + sums[1][::-1]
    return total.astype(jnp.bfloat16)
```

```python
import jax
import jax.numpy as jnp
from jax import lax
from jax.sharding import PartitionSpec as P


def section_grad_v(query_rows, key_rows, grad_rows, segs):
    length = query_rows.shape[0]
    scores = jnp.dot(query_rows, key_rows.T, preferred_element_type=jnp.float32) / jnp.sqrt(
        jnp.float32(query_rows.shape[1])
    )
    position = jnp.arange(length, dtype=jnp.int32)
    keep = (position[None, :] <= position[:, None]) & (segs[None, :] == segs[:, None])
    masked = jnp.where(keep, scores, jnp.float32(-1e30))
    top = jnp.max(masked, axis=1, keepdims=True)
    weights = jnp.where(keep, jnp.exp(masked - top), jnp.float32(0.0))
    probs = (weights / jnp.sum(weights, axis=1, keepdims=True)).astype(jnp.bfloat16)
    return jnp.einsum("qk,qd->kd", probs, grad_rows, preferred_element_type=jnp.float32).astype(
        jnp.bfloat16
    )


def body(activations, queries, keys, grad_out, segment_ids):
    ways = lax.axis_size("dp")
    slots = lax.axis_size("pipe")
    chips = ways // 2
    me = lax.axis_index("dp")
    width = activations.shape[3] // ways
    grads = [
        section_grad_v(queries[h, 0], keys[h, 0], grad_out[h, 0], segment_ids[h, 0, 0])
        for h in range(2)
    ]

    def part(half, owner):
        acts = lax.dynamic_slice_in_dim(activations[half, 0], owner * width, width, axis=1)
        return jnp.einsum("te,td->ed", grads[half], acts, preferred_element_type=jnp.float32)

    def swap(block, distance):
        return lax.ppermute(block, "dp", [(i, i ^ distance) for i in range(ways)])

    def mirror(block):
        return lax.ppermute(block, "pipe", [(i, slots - 1 - i) for i in range(slots)])

    total = [None] * chips
    for r in reversed(range(chips)):
        owner = me ^ (2 * r)
        got = swap(jnp.stack([part(1, owner ^ 1), part(0, owner ^ 1)]), 1)
        moved = mirror(part(1, owner) + got[0])
        total[r] = part(0, owner) + got[1] + moved
    for r in reversed(range(1, chips)):
        low = r & -r
        total[r ^ low] = total[r ^ low] + swap(total[r], 2 * low)
    return total[0].T.astype(jnp.bfloat16)[None]


def solution(mesh):
    spec = P(None, "pipe", "dp", None)
    return jax.shard_map(
        body,
        mesh=mesh,
        in_specs=(spec,) * 5,
        out_specs=P("pipe", "dp", None),
        check_vma=False,
    )
```

```python
import functools

import jax
import jax.numpy as jnp
from jax import lax
from jax.experimental import pallas as pl
from jax.experimental.pallas import tpu as pltpu
from jax.sharding import PartitionSpec as P

VMEM = pl.BlockSpec(memory_space=pltpu.VMEM)
SMALL = pltpu.CompilerParams(vmem_limit_bytes=8 << 20)


def grad_v_columns(query_rows, key_rows, grad_rows, segs):
    length, head = query_rows.shape
    scores = lax.dot_general(
        query_rows, key_rows, (((1,), (1,)), ((), ())), preferred_element_type=jnp.float32
    ) / jnp.sqrt(jnp.float32(head))
    shape = (length, length)
    across = jnp.broadcast_to(segs, shape)
    keep = (across == across.T) & (
        lax.broadcasted_iota(jnp.int32, shape, 1) <= lax.broadcasted_iota(jnp.int32, shape, 0)
    )
    masked = jnp.where(keep, scores, jnp.float32(-1e30))
    top = jnp.max(masked, axis=1, keepdims=True)
    weights = jnp.where(keep, jnp.exp(masked - top), jnp.float32(0.0))
    probs = (weights / jnp.sum(weights, axis=1, keepdims=True)).astype(jnp.bfloat16)
    return lax.dot_general(
        grad_rows, probs, (((0,), (0,)), ((), ())), preferred_element_type=jnp.float32
    ).astype(jnp.bfloat16)


def block_columns(flip, width):
    owner = lax.axis_index("dp") ^ flip
    return pl.ds(pl.multiple_of(owner * width, 128), width)


def front_kernel(flip, width, acts, queries, keys, grad_out, segs, grads, first, *scratch):
    columns, ready = scratch[0], scratch[-1]
    sources = [queries, keys, grad_out, segs, acts.at[1, 0, :, block_columns(flip, width)]]
    holders = [*scratch[1:-1], columns]
    copies = [
        pltpu.make_async_copy(source, holder, ready.at[i])
        for i, (source, holder) in enumerate(zip(sources, holders))
    ]
    for copy in copies:
        copy.start()
    for copy in copies[:-1]:
        copy.wait()
    query_rows, key_rows, grad_rows, seg_rows = scratch[1:-1]
    for half in (1, 0):
        grads[half] = grad_v_columns(
            query_rows[half, 0], key_rows[half, 0], grad_rows[half, 0], seg_rows[half, 0]
        )
    copies[-1].wait()
    first[0] = jnp.dot(grads[1], columns[...], preferred_element_type=jnp.float32)


def front(activations, queries, keys, grad_out, segment_ids, flip, width):
    head, length = queries.shape[3], queries.shape[2]
    if width % 128:
        grads = jnp.stack(
            [
                grad_v_columns(
                    queries[h, 0], keys[h, 0], grad_out[h, 0], segment_ids[h, 0]
                )
                for h in range(2)
            ]
        )
        return grads, *plain_blocks(activations, grads, width, [[[(DOT, 1, flip)]]])
    small = (queries, keys, grad_out, segment_ids)
    return pl.pallas_call(
        functools.partial(front_kernel, flip, width),
        out_shape=(
            jax.ShapeDtypeStruct((2, head, length), jnp.bfloat16),
            jax.ShapeDtypeStruct((1, head, width), jnp.float32),
        ),
        in_specs=[pl.BlockSpec(memory_space=pltpu.HBM)] * 5,
        out_specs=(VMEM, VMEM),
        scratch_shapes=[
            pltpu.VMEM((length, width), activations.dtype),
            *(pltpu.VMEM(value.shape, value.dtype) for value in small),
            pltpu.SemaphoreType.DMA((5,)),
        ],
        compiler_params=SMALL,
        name="front",
    )(activations, *small)


def plain_blocks(acts, grads, width, plan):
    def slab(terms):
        value = None
        for term in terms:
            if term[0] is DOT:
                owner = lax.axis_index("dp") ^ term[2]
                columns = lax.dynamic_slice_in_dim(acts[term[1], 0], owner * width, width, axis=1)
                term = jnp.dot(grads[term[1]], columns, preferred_element_type=jnp.float32)
            else:
                term = term[0][term[1]]
            value = term if value is None else value + term
        return value

    return tuple(jnp.stack([slab(terms) for terms in slabs]) for slabs in plan)


def blocks_kernel(plan, count, width, *refs):
    outs = refs[count:]
    acts, grads = refs[0], refs[1]
    for out, slabs in zip(outs, plan):
        for place, (dots, adds) in enumerate(slabs):
            value = None
            for half, flip in dots:
                term = jnp.dot(
                    grads[half],
                    acts[half, 0, :, block_columns(flip, width)],
                    preferred_element_type=jnp.float32,
                )
                value = term if value is None else value + term
            for operand, slab in adds:
                term = refs[operand][slab]
                value = term if value is None else value + term
            out[place] = value


def blocks(name, acts, grads, width, plan):
    if width % 128:
        return plain_blocks(acts, grads, width, plan)
    operands = [acts, grads]
    numbers = {}
    static = []
    for slabs in plan:
        made = []
        for terms in slabs:
            dots = tuple(term[1:] for term in terms if term[0] is DOT)
            adds = []
            for term in terms:
                if term[0] is not DOT:
                    if id(term[0]) not in numbers:
                        numbers[id(term[0])] = len(operands)
                        operands.append(term[0])
                    adds.append((numbers[id(term[0])], term[1]))
            made.append((dots, tuple(adds)))
        static.append(tuple(made))
    head = grads.shape[1]
    return pl.pallas_call(
        functools.partial(blocks_kernel, tuple(static), len(operands), width),
        out_shape=tuple(
            jax.ShapeDtypeStruct((len(slabs), head, width), jnp.float32) for slabs in static
        ),
        in_specs=[VMEM] * len(operands),
        out_specs=tuple(VMEM for _ in static),
        compiler_params=SMALL,
        name=name,
    )(*operands)


DOT = object()


def finish_kernel(count, *refs):
    out = refs[count]
    for low in range(0, out.shape[1], 128):
        value = refs[0][0, :, low : low + 128]
        for ref in refs[1:count]:
            value = value + ref[0, :, low : low + 128]
        out[0, low : low + 128, :] = value.T.astype(out.dtype)


def finish(terms):
    head, width = terms[0].shape[1:]
    if width % 128:
        return functools.reduce(jnp.add, terms).swapaxes(1, 2).astype(jnp.bfloat16)
    return pl.pallas_call(
        functools.partial(finish_kernel, len(terms)),
        out_shape=jax.ShapeDtypeStruct((1, width, head), jnp.bfloat16),
        in_specs=[VMEM] * len(terms),
        out_specs=VMEM,
        compiler_params=SMALL,
        name="finish",
    )(*terms)


def body(activations, queries, keys, grad_out, segment_ids):
    ways = lax.axis_size("dp")
    slots = lax.axis_size("pipe")
    chips = ways // 2
    width = activations.shape[3] // ways

    def swap(block, distance):
        return lax.ppermute(block, "dp", [(i, i ^ distance) for i in range(ways)])

    def mirror(block):
        return lax.ppermute(block, "pipe", [(i, slots - 1 - i) for i in range(slots)])

    last = chips - 1
    grads, first = front(
        activations, queries, keys, grad_out, segment_ids, 2 * last + 1, width
    )
    make = functools.partial(blocks, acts=activations, grads=grads, width=width)
    order = list(reversed(range(chips)))
    got_upper = {last: swap(first, 1)}
    got_lower = {}
    for r in order:
        plan = [[[(DOT, 0, 2 * r + 1)]]]
        if r != last:
            plan.append([[(DOT, 1, 2 * r + 1)]])
        sent = make("theirs", plan=plan)
        got_lower[r] = swap(sent[0], 1)
        if r != last:
            got_upper[r] = swap(sent[1], 1)
    moved = {}
    for r in order:
        (upper,) = make("upper", plan=[[[(DOT, 1, 2 * r), (got_upper[r], 0)]]])
        moved[r] = mirror(upper)
    terms = {r: [(DOT, 0, 2 * r), (got_lower[r], 0), (moved[r], 0)] for r in order}
    (base,) = make("base", plan=[[terms[0][:2]]])
    terms[0] = [(base, 0), terms[0][2]]
    for r in order[:-1]:
        (total,) = make("lower", plan=[[terms[r]]])
        low = r & -r
        terms[r ^ low].append((swap(total, 2 * low), 0))
    return finish([term[0] for term in terms[0]])


def solution(mesh):
    spec = P(None, "pipe", "dp", None)
    return jax.shard_map(
        body,
        mesh=mesh,
        in_specs=(spec,) * 5,
        out_specs=P("pipe", "dp", None),
        check_vma=False,
    )
```

```python
import functools

import jax
import jax.numpy as jnp
from jax import lax
from jax.experimental import pallas as pl
from jax.experimental.pallas import tpu as pltpu
from jax.sharding import PartitionSpec as P

VMEM = pl.BlockSpec(memory_space=pltpu.VMEM)
SMALL = pltpu.CompilerParams(vmem_limit_bytes=8 << 20)


def grad_v_columns(query_rows, key_rows, grad_rows, segs):
    length, head = query_rows.shape
    scores = lax.dot_general(
        query_rows, key_rows, (((1,), (1,)), ((), ())), preferred_element_type=jnp.float32
    ) / jnp.sqrt(jnp.float32(head))
    shape = (length, length)
    across = jnp.broadcast_to(segs, shape)
    keep = (across == across.T) & (
        lax.broadcasted_iota(jnp.int32, shape, 1) <= lax.broadcasted_iota(jnp.int32, shape, 0)
    )
    masked = jnp.where(keep, scores, jnp.float32(-1e30))
    top = jnp.max(masked, axis=1, keepdims=True)
    weights = jnp.where(keep, jnp.exp(masked - top), jnp.float32(0.0))
    probs = (weights / jnp.sum(weights, axis=1, keepdims=True)).astype(jnp.bfloat16)
    return lax.dot_general(
        grad_rows, probs, (((0,), (0,)), ((), ())), preferred_element_type=jnp.float32
    ).astype(jnp.bfloat16)


def block_columns(flip, width):
    owner = lax.axis_index("dp") ^ flip
    return pl.ds(pl.multiple_of(owner * width, 128), width)


def front_kernel(flip, width, acts, queries, keys, grad_out, segs, grads, first, *scratch):
    columns, ready = scratch[0], scratch[-1]
    sources = [queries, keys, grad_out, segs, acts.at[1, 0, :, block_columns(flip, width)]]
    holders = [*scratch[1:-1], columns]
    copies = [
        pltpu.make_async_copy(source, holder, ready.at[i])
        for i, (source, holder) in enumerate(zip(sources, holders))
    ]
    for copy in copies:
        copy.start()
    for copy in copies[:-1]:
        copy.wait()
    query_rows, key_rows, grad_rows, seg_rows = scratch[1:-1]
    for half in (1, 0):
        grads[half] = grad_v_columns(
            query_rows[half, 0], key_rows[half, 0], grad_rows[half, 0], seg_rows[half, 0]
        )
    copies[-1].wait()
    first[0] = jnp.dot(grads[1], columns[...], preferred_element_type=jnp.float32)


def front(activations, queries, keys, grad_out, segment_ids, flip, width):
    head, length = queries.shape[3], queries.shape[2]
    if width % 128:
        grads = jnp.stack(
            [
                grad_v_columns(
                    queries[h, 0], keys[h, 0], grad_out[h, 0], segment_ids[h, 0]
                )
                for h in range(2)
            ]
        )
        return grads, *plain_blocks(activations, grads, width, [[[(DOT, 1, flip)]]])
    small = (queries, keys, grad_out, segment_ids)
    return pl.pallas_call(
        functools.partial(front_kernel, flip, width),
        out_shape=(
            jax.ShapeDtypeStruct((2, head, length), jnp.bfloat16),
            jax.ShapeDtypeStruct((1, head, width), jnp.float32),
        ),
        in_specs=[pl.BlockSpec(memory_space=pltpu.HBM)] * 5,
        out_specs=(VMEM, VMEM),
        scratch_shapes=[
            pltpu.VMEM((length, width), activations.dtype),
            *(pltpu.VMEM(value.shape, value.dtype) for value in small),
            pltpu.SemaphoreType.DMA((5,)),
        ],
        compiler_params=SMALL,
        name="front",
    )(*(pltpu.with_memory_space_constraint(x, pltpu.HBM) for x in (activations, *small)))


def plain_blocks(acts, grads, width, plan):
    def slab(terms):
        value = None
        for term in terms:
            if term[0] is DOT:
                owner = lax.axis_index("dp") ^ term[2]
                columns = lax.dynamic_slice_in_dim(acts[term[1], 0], owner * width, width, axis=1)
                term = jnp.dot(grads[term[1]], columns, preferred_element_type=jnp.float32)
            else:
                term = term[0][term[1]]
            value = term if value is None else value + term
        return value

    return tuple(jnp.stack([slab(terms) for terms in slabs]) for slabs in plan)


def blocks_kernel(plan, count, width, *refs):
    outs = refs[count:]
    acts, grads = refs[0], refs[1]
    for out, slabs in zip(outs, plan):
        for place, (dots, adds) in enumerate(slabs):
            value = None
            for half, flip in dots:
                term = jnp.dot(
                    grads[half],
                    acts[half, 0, :, block_columns(flip, width)],
                    preferred_element_type=jnp.float32,
                )
                value = term if value is None else value + term
            for operand, slab in adds:
                term = refs[operand][slab]
                value = term if value is None else value + term
            out[place] = value


def blocks(name, acts, grads, width, plan):
    if width % 128:
        return plain_blocks(acts, grads, width, plan)
    operands = [acts, grads]
    numbers = {}
    static = []
    for slabs in plan:
        made = []
        for terms in slabs:
            dots = tuple(term[1:] for term in terms if term[0] is DOT)
            adds = []
            for term in terms:
                if term[0] is not DOT:
                    if id(term[0]) not in numbers:
                        numbers[id(term[0])] = len(operands)
                        operands.append(term[0])
                    adds.append((numbers[id(term[0])], term[1]))
            made.append((dots, tuple(adds)))
        static.append(tuple(made))
    head = grads.shape[1]
    return pl.pallas_call(
        functools.partial(blocks_kernel, tuple(static), len(operands), width),
        out_shape=tuple(
            jax.ShapeDtypeStruct((len(slabs), head, width), jnp.float32) for slabs in static
        ),
        in_specs=[VMEM] * len(operands),
        out_specs=tuple(VMEM for _ in static),
        compiler_params=SMALL,
        name=name,
    )(*operands)


DOT = object()


def finish_kernel(count, *refs):
    out = refs[count]
    for low in range(0, out.shape[1], 128):
        value = refs[0][0, :, low : low + 128]
        for ref in refs[1:count]:
            value = value + ref[0, :, low : low + 128]
        out[0, low : low + 128, :] = value.T.astype(out.dtype)


def finish(terms):
    head, width = terms[0].shape[1:]
    if width % 128:
        return functools.reduce(jnp.add, terms).swapaxes(1, 2).astype(jnp.bfloat16)
    return pl.pallas_call(
        functools.partial(finish_kernel, len(terms)),
        out_shape=jax.ShapeDtypeStruct((1, width, head), jnp.bfloat16),
        in_specs=[VMEM] * len(terms),
        out_specs=VMEM,
        compiler_params=SMALL,
        name="finish",
    )(*terms)


def body(activations, queries, keys, grad_out, segment_ids):
    ways = lax.axis_size("dp")
    slots = lax.axis_size("pipe")
    chips = ways // 2
    width = activations.shape[3] // ways

    def swap(block, distance):
        return lax.ppermute(block, "dp", [(i, i ^ distance) for i in range(ways)])

    def mirror(block):
        return lax.ppermute(block, "pipe", [(i, slots - 1 - i) for i in range(slots)])

    last = chips - 1
    grads, first = front(
        activations, queries, keys, grad_out, segment_ids, 2 * last + 1, width
    )
    make = functools.partial(blocks, acts=activations, grads=grads, width=width)
    order = list(reversed(range(chips)))
    got_upper = {last: swap(first, 1)}
    got_lower = {}
    for r in order:
        plan = [[[(DOT, 0, 2 * r + 1)]]]
        if r != last:
            plan.append([[(DOT, 1, 2 * r + 1)]])
        sent = make("theirs", plan=plan)
        got_lower[r] = swap(sent[0], 1)
        if r != last:
            got_upper[r] = swap(sent[1], 1)
    moved = {}
    for r in order:
        (upper,) = make("upper", plan=[[[(DOT, 1, 2 * r), (got_upper[r], 0)]]])
        moved[r] = mirror(upper)
    terms = {r: [(DOT, 0, 2 * r), (got_lower[r], 0), (moved[r], 0)] for r in order}
    (base,) = make("base", plan=[[terms[0][:2]]])
    terms[0] = [(base, 0), terms[0][2]]
    for r in order[:-1]:
        (total,) = make("lower", plan=[[terms[r]]])
        low = r & -r
        terms[r ^ low].append((swap(total, 2 * low), 0))
    return finish([term[0] for term in terms[0]])


def solution(mesh):
    spec = P(None, "pipe", "dp", None)
    return jax.shard_map(
        body,
        mesh=mesh,
        in_specs=(spec,) * 5,
        out_specs=P("pipe", "dp", None),
        check_vma=False,
    )
```

```python
import functools

import jax
import jax.numpy as jnp
from jax import lax
from jax.experimental import pallas as pl
from jax.experimental.pallas import tpu as pltpu
from jax.sharding import PartitionSpec as P

VMEM = pl.BlockSpec(memory_space=pltpu.VMEM)
SOON = pl.CostEstimate(flops=25_000_000_000, bytes_accessed=1000, transcendentals=0)
SMALL = pltpu.CompilerParams(vmem_limit_bytes=8 << 20)


def grad_v_columns(query_rows, key_rows, grad_rows, segs):
    length, head = query_rows.shape
    scores = lax.dot_general(
        query_rows, key_rows, (((1,), (1,)), ((), ())), preferred_element_type=jnp.float32
    ) / jnp.sqrt(jnp.float32(head))
    shape = (length, length)
    across = jnp.broadcast_to(segs, shape)
    keep = (across == across.T) & (
        lax.broadcasted_iota(jnp.int32, shape, 1) <= lax.broadcasted_iota(jnp.int32, shape, 0)
    )
    masked = jnp.where(keep, scores, jnp.float32(-1e30))
    top = jnp.max(masked, axis=1, keepdims=True)
    weights = jnp.where(keep, jnp.exp(masked - top), jnp.float32(0.0))
    probs = (weights / jnp.sum(weights, axis=1, keepdims=True)).astype(jnp.bfloat16)
    return lax.dot_general(
        grad_rows, probs, (((0,), (0,)), ((), ())), preferred_element_type=jnp.float32
    ).astype(jnp.bfloat16)


def block_columns(flip, width):
    owner = lax.axis_index("dp") ^ flip
    return pl.ds(pl.multiple_of(owner * width, 128), width)


def front_kernel(flip, width, acts, queries, keys, grad_out, segs, grads, first, *scratch):
    columns, ready = scratch[0], scratch[-1]
    sources = [queries, keys, grad_out, segs, acts.at[:, 0, :, block_columns(flip, width)]]
    holders = [*scratch[1:-1], columns]
    copies = [
        pltpu.make_async_copy(source, holder, ready.at[i])
        for i, (source, holder) in enumerate(zip(sources, holders))
    ]
    for copy in copies:
        copy.start()
    for copy in copies[:-1]:
        copy.wait()
    query_rows, key_rows, grad_rows, seg_rows = scratch[1:-1]
    for half in (1, 0):
        grads[half] = grad_v_columns(
            query_rows[half, 0], key_rows[half, 0], grad_rows[half, 0], seg_rows[half, 0]
        )
    copies[-1].wait()
    for slab in range(2):
        first[slab] = jnp.dot(grads[1 - slab], columns[1 - slab], preferred_element_type=jnp.float32)


def front(activations, queries, keys, grad_out, segment_ids, flip, width):
    head, length = queries.shape[3], queries.shape[2]
    if width % 128:
        grads = jnp.stack(
            [
                grad_v_columns(queries[h, 0], keys[h, 0], grad_out[h, 0], segment_ids[h, 0])
                for h in range(2)
            ]
        )
        return grads, *plain_blocks(
            activations,
            grads,
            width,
            [[(slab, 0, head, [(DOT, 1 - slab, flip, 0)]) for slab in range(2)]],
        )
    small = (queries, keys, grad_out, segment_ids)
    return pl.pallas_call(
        functools.partial(front_kernel, flip, width),
        out_shape=(
            jax.ShapeDtypeStruct((2, head, length), jnp.bfloat16),
            jax.ShapeDtypeStruct((2, head, width), jnp.float32),
        ),
        in_specs=[pl.BlockSpec(memory_space=pltpu.HBM)] * 5,
        out_specs=(VMEM, VMEM),
        scratch_shapes=[
            pltpu.VMEM((2, length, width), activations.dtype),
            *(pltpu.VMEM(value.shape, value.dtype) for value in small),
            pltpu.SemaphoreType.DMA((5,)),
        ],
        compiler_params=SMALL,
        cost_estimate=SOON,
        name="front",
    )(*(pltpu.with_memory_space_constraint(x, pltpu.HBM) for x in (activations, *small)))


def extent(segments):
    slabs = max(slab for slab, _, _, _ in segments) + 1
    return slabs, max(low + rows for _, low, rows, _ in segments)


def plain_blocks(acts, grads, width, plan):
    outs = []
    for segments in plan:
        out = jnp.zeros((*extent(segments), width), jnp.float32)
        for slab, low, rows, terms in segments:
            value = None
            for term in terms:
                if term[0] is DOT:
                    _, half, flip, head_low = term
                    owner = lax.axis_index("dp") ^ flip
                    columns = lax.dynamic_slice_in_dim(acts[half, 0], owner * width, width, axis=1)
                    term = jnp.dot(
                        grads[half, head_low : head_low + rows],
                        columns,
                        preferred_element_type=jnp.float32,
                    )
                else:
                    array, place, first = term
                    term = array[place, first : first + rows]
                value = term if value is None else value + term
            out = out.at[slab, low : low + rows].set(value)
        outs.append(out)
    return tuple(outs)


def blocks_kernel(plan, count, width, *refs):
    acts, grads = refs[0], refs[1]
    refs[-1][...] = jnp.zeros_like(refs[-1])
    for out, segments in zip(refs[count:-1], plan):
        for slab, low, rows, terms in segments:
            value = None
            for term in terms:
                if term[0] is DOT:
                    _, half, flip, head_low = term
                    term = jnp.dot(
                        grads[half, head_low : head_low + rows, :],
                        acts[half, 0, :, block_columns(flip, width)],
                        preferred_element_type=jnp.float32,
                    )
                else:
                    operand, place, first = term
                    term = refs[operand][place, first : first + rows, :]
                value = term if value is None else value + term
            out[slab, low : low + rows, :] = value


def number_operands(plan, operands):
    numbers = {}

    def numbered(term):
        if term[0] is DOT:
            return term
        if id(term[0]) not in numbers:
            numbers[id(term[0])] = len(operands)
            operands.append(term[0])
        return (numbers[id(term[0])], *term[1:])

    return [
        [(slab, low, rows, [numbered(term) for term in terms]) for slab, low, rows, terms in segments]
        for segments in plan
    ]


def blocks(name, acts, grads, width, plan, token):
    if width % 128:
        return *plain_blocks(acts, grads, width, plan), None
    operands = [acts, grads]
    static = number_operands(plan, operands)
    if token is not None:
        operands.append(token)
    shapes = [(*extent(segments), width) for segments in static] + [(8, 128)]
    return pl.pallas_call(
        functools.partial(blocks_kernel, static, len(operands), width),
        out_shape=tuple(jax.ShapeDtypeStruct(shape, jnp.float32) for shape in shapes),
        in_specs=[VMEM] * len(operands),
        out_specs=(VMEM,) * len(shapes),
        compiler_params=SMALL,
        cost_estimate=SOON,
        name=name,
    )(*operands)


DOT = object()


def finish_kernel(segments, count, *refs):
    out = refs[count]
    for left in range(0, out.shape[1], 128):
        rows_of = []
        for _, _, rows, terms in segments:
            value = None
            for operand, place, first in terms:
                term = refs[operand][place, first : first + rows, left : left + 128]
                value = term if value is None else value + term
            rows_of.append(value)
        value = jnp.concatenate(rows_of, axis=0) if len(rows_of) > 1 else rows_of[0]
        out[0, left : left + 128, :] = value.T.astype(out.dtype)


def finish(segments, head, width):
    if width % 128:
        (value,) = plain_blocks(None, None, width, [segments])
        return value.swapaxes(1, 2).astype(jnp.bfloat16)
    operands = []
    (static,) = number_operands([segments], operands)
    return pl.pallas_call(
        functools.partial(finish_kernel, static, len(operands)),
        out_shape=jax.ShapeDtypeStruct((1, width, head), jnp.bfloat16),
        in_specs=[VMEM] * len(operands),
        out_specs=VMEM,
        compiler_params=SMALL,
        cost_estimate=SOON,
        name="finish",
    )(*operands)


class Section:
    def __init__(self, half, chips):
        self.half = half
        self.dots = [True] * chips
        self.given = [[] for _ in range(chips)]

    def add(self, block, low, high, array, slab=0):
        self.given[block].append((low, high, array, slab, low))

    def settle(self, block, low, high, array, slab=0):
        kept = []
        for first, last, other, place, top in self.given[block]:
            for start, stop in ((first, min(last, low)), (max(first, high), last)):
                if start < stop:
                    kept.append((start, stop, other, place, top))
        self.given[block] = kept
        self.add(block, low, high, array, slab)

    def segments(self, block, low, high, slab=0):
        edges = {low, high}
        for start, stop, *_ in self.given[block]:
            edges |= {start, stop}
        edges = sorted(edge for edge in edges if low <= edge <= high)
        made = []
        for start, stop in zip(edges, edges[1:]):
            terms = [(DOT, self.half, 2 * block, start)] if self.dots[block] else []
            terms += [
                (array, place, start - top)
                for first, last, array, place, top in self.given[block]
                if first <= start and stop <= last
            ]
            made.append((slab, start - low, stop - start, terms))
        return made


def order(chips, head):
    last = chips - 1
    cut, half = head * 5 // 8, head // 2
    pairs = [(1, block) for block in reversed(range(last))]
    pairs += [(0, block) for block in reversed(range(last))]
    everything = list(reversed(range(chips)))
    if chips < 4:
        events = [("core", *pairs)] if pairs else []
        events += [("up", block, 0, head) for block in everything] + [("base", *everything)]
        return events + [("down", block, 0, head) for block in everything[:-1]]
    events = [
        ("core", *pairs),
        ("up", last, 0, cut),
        ("raw", last, cut, head),
        ("up", last - 1, 0, cut),
        ("up", 1, 0, half),
        ("base", *everything),
        ("down", last, 0, cut),
        ("up", last - 1, cut, head),
    ]
    for block in reversed(range(2, last - 1)):
        events += [("up", block, 0, head), ("down", block + 1, 0, head)]
    return [
        *events,
        ("up", 1, half, head),
        ("down", 1, 0, half),
        ("down", 2, 0, head),
        ("up", 0, 0, head),
        ("down", 1, half, head),
    ]


def body(activations, queries, keys, grad_out, segment_ids):
    ways = lax.axis_size("dp")
    slots = lax.axis_size("pipe")
    chips = ways // 2
    head = queries.shape[3]
    width = activations.shape[3] // ways
    last = chips - 1

    def swap(block, distance):
        return lax.ppermute(block, "dp", [(i, i ^ distance) for i in range(ways)])

    def mirror(block):
        return lax.ppermute(block, "pipe", [(i, slots - 1 - i) for i in range(slots)])

    grads, first = front(
        activations, queries, keys, grad_out, segment_ids, 2 * last + 1, width
    )
    lower, upper = Section(0, chips), Section(1, chips)
    got = swap(first, 1)
    for section in (upper, lower):
        section.add(last, 0, head, got, 1 - section.half)
    token = None

    def make(name, plan):
        nonlocal token
        *made, token = blocks(name, activations, grads, width, plan, token)
        return made

    def exchange(wanted):
        plan = [
            (slab, 0, head, [(DOT, section.half, 2 * block + 1, 0)])
            for slab, (section, block) in enumerate(wanted)
        ]
        got = swap(make("theirs", [plan])[0], 1)
        for slab, (section, block) in enumerate(wanted):
            section.add(block, 0, head, got, slab)

    def send_up(block, low, high):
        (part,) = make("upper", [upper.segments(block, low, high)])
        return mirror(part)

    def send_raw(block, low, high):
        rows = (block, low, high)
        (both,) = make("raw", [upper.segments(*rows, 0) + lower.segments(*rows, 1)])
        bit = block & -block
        got = swap(both, 2 * bit)
        upper.add(block ^ bit, low, high, got, 0)
        lower.add(block ^ bit, low, high, got, 1)

    def send_down(block, low, high):
        (part,) = make("lower", [lower.segments(block, low, high)])
        bit = block & -block
        lower.add(block ^ bit, low, high, swap(part, 2 * bit))

    def settle(blocks_of):
        sums = make("base", [lower.segments(block, 0, head) for block in blocks_of])
        for block, array in zip(blocks_of, sums):
            lower.dots[block] = False
            lower.settle(block, 0, head, array)

    def take(block, low, high):
        (part,) = make("take", [lower.segments(block, low, high)])
        lower.settle(block, low, high, part)

    late = {}

    def arrive(block, low, high):
        for rows in [rows for rows in late if rows[0] == block]:
            if low <= rows[1] and rows[2] <= high:
                lower.add(*rows, late.pop(rows))

    for event, *what in order(chips, head):
        if event == "core":
            exchange([(upper if half else lower, block) for half, block in what])
        elif event == "base":
            settle(what)
        elif event == "up":
            late[tuple(what)] = send_up(*what)
        elif event == "raw":
            send_raw(*what)
        elif event == "down":
            arrive(*what)
            send_down(*what)
        elif event == "take":
            arrive(*what)
            take(*what)
    arrive(0, 0, head)
    assert not late
    return finish(lower.segments(0, 0, head), head, width)


def solution(mesh):
    spec = P(None, "pipe", "dp", None)
    return jax.shard_map(
        body,
        mesh=mesh,
        in_specs=(spec,) * 5,
        out_specs=P("pipe", "dp", None),
        check_vma=False,
    )
```

```python
import functools

import jax
import jax.numpy as jnp
from jax import lax
from jax.experimental import pallas as pl
from jax.experimental.pallas import tpu as pltpu
from jax.sharding import PartitionSpec as P

VMEM = pl.BlockSpec(memory_space=pltpu.VMEM)
SOON = pl.CostEstimate(flops=10_000_000_000, bytes_accessed=1000, transcendentals=0)
SMALL = pltpu.CompilerParams(vmem_limit_bytes=8 << 20)


def grad_v_columns(query_rows, key_rows, grad_rows, segs):
    length, head = query_rows.shape
    scores = lax.dot_general(
        query_rows, key_rows, (((1,), (1,)), ((), ())), preferred_element_type=jnp.float32
    ) / jnp.sqrt(jnp.float32(head))
    shape = (length, length)
    across = jnp.broadcast_to(segs, shape)
    keep = (across == across.T) & (
        lax.broadcasted_iota(jnp.int32, shape, 1) <= lax.broadcasted_iota(jnp.int32, shape, 0)
    )
    masked = jnp.where(keep, scores, jnp.float32(-1e30))
    top = jnp.max(masked, axis=1, keepdims=True)
    weights = jnp.where(keep, jnp.exp(masked - top), jnp.float32(0.0))
    probs = (weights / jnp.sum(weights, axis=1, keepdims=True)).astype(jnp.bfloat16)
    return lax.dot_general(
        grad_rows, probs, (((0,), (0,)), ((), ())), preferred_element_type=jnp.float32
    ).astype(jnp.bfloat16)


def block_columns(flip, width):
    owner = lax.axis_index("dp") ^ flip
    return pl.ds(pl.multiple_of(owner * width, 128), width)


def front_kernel(flip, width, acts, queries, keys, grad_out, segs, grads, first, *scratch):
    columns, ready = scratch[0], scratch[-1]
    sources = [queries, keys, grad_out, segs, acts.at[:, 0, :, block_columns(flip, width)]]
    holders = [*scratch[1:-1], columns]
    copies = [
        pltpu.make_async_copy(source, holder, ready.at[i])
        for i, (source, holder) in enumerate(zip(sources, holders))
    ]
    for copy in copies:
        copy.start()
    for copy in copies[:-1]:
        copy.wait()
    query_rows, key_rows, grad_rows, seg_rows = scratch[1:-1]
    for half in (1, 0):
        grads[half] = grad_v_columns(
            query_rows[half, 0], key_rows[half, 0], grad_rows[half, 0], seg_rows[half, 0]
        )
    copies[-1].wait()
    for slab in range(2):
        first[slab] = jnp.dot(grads[1 - slab], columns[1 - slab], preferred_element_type=jnp.float32)


def front(activations, queries, keys, grad_out, segment_ids, flip, width):
    head, length = queries.shape[3], queries.shape[2]
    if width % 128:
        grads = jnp.stack(
            [
                grad_v_columns(queries[h, 0], keys[h, 0], grad_out[h, 0], segment_ids[h, 0])
                for h in range(2)
            ]
        )
        return grads, *plain_blocks(
            activations,
            grads,
            width,
            [[(slab, 0, head, [(DOT, 1 - slab, flip, 0)]) for slab in range(2)]],
        )
    small = (queries, keys, grad_out, segment_ids)
    return pl.pallas_call(
        functools.partial(front_kernel, flip, width),
        out_shape=(
            jax.ShapeDtypeStruct((2, head, length), jnp.bfloat16),
            jax.ShapeDtypeStruct((2, head, width), jnp.float32),
        ),
        in_specs=[pl.BlockSpec(memory_space=pltpu.HBM)] * 5,
        out_specs=(VMEM, VMEM),
        scratch_shapes=[
            pltpu.VMEM((2, length, width), activations.dtype),
            *(pltpu.VMEM(value.shape, value.dtype) for value in small),
            pltpu.SemaphoreType.DMA((5,)),
        ],
        compiler_params=SMALL,
        cost_estimate=SOON,
        name="front",
    )(*(pltpu.with_memory_space_constraint(x, pltpu.HBM) for x in (activations, *small)))


def extent(segments):
    slabs = max(slab for slab, _, _, _ in segments) + 1
    return slabs, max(low + rows for _, low, rows, _ in segments)


def plain_blocks(acts, grads, width, plan):
    outs = []
    for segments in plan:
        out = jnp.zeros((*extent(segments), width), jnp.float32)
        for slab, low, rows, terms in segments:
            value = None
            for term in terms:
                if term[0] is DOT:
                    _, half, flip, head_low = term
                    owner = lax.axis_index("dp") ^ flip
                    columns = lax.dynamic_slice_in_dim(acts[half, 0], owner * width, width, axis=1)
                    term = jnp.dot(
                        grads[half, head_low : head_low + rows],
                        columns,
                        preferred_element_type=jnp.float32,
                    )
                else:
                    array, place, first = term
                    term = array[place, first : first + rows]
                value = term if value is None else value + term
            out = out.at[slab, low : low + rows].set(value)
        outs.append(out)
    return tuple(outs)


def blocks_kernel(plan, count, width, *refs):
    acts, grads = refs[0], refs[1]
    refs[-1][...] = jnp.zeros_like(refs[-1])
    for out, segments in zip(refs[count:-1], plan):
        for slab, low, rows, terms in segments:
            value = None
            for term in terms:
                if term[0] is DOT:
                    _, half, flip, head_low = term
                    term = jnp.dot(
                        grads[half, head_low : head_low + rows, :],
                        acts[half, 0, :, block_columns(flip, width)],
                        preferred_element_type=jnp.float32,
                    )
                else:
                    operand, place, first = term
                    term = refs[operand][place, first : first + rows, :]
                value = term if value is None else value + term
            out[slab, low : low + rows, :] = value


def number_operands(plan, operands):
    numbers = {}

    def numbered(term):
        if term[0] is DOT:
            return term
        if id(term[0]) not in numbers:
            numbers[id(term[0])] = len(operands)
            operands.append(term[0])
        return (numbers[id(term[0])], *term[1:])

    return [
        [(slab, low, rows, [numbered(term) for term in terms]) for slab, low, rows, terms in segments]
        for segments in plan
    ]


def blocks(name, acts, grads, width, plan, token):
    if width % 128:
        return *plain_blocks(acts, grads, width, plan), None
    operands = [acts, grads]
    static = number_operands(plan, operands)
    if token is not None:
        operands.append(token)
    shapes = [(*extent(segments), width) for segments in static] + [(8, 128)]
    return pl.pallas_call(
        functools.partial(blocks_kernel, static, len(operands), width),
        out_shape=tuple(jax.ShapeDtypeStruct(shape, jnp.float32) for shape in shapes),
        in_specs=[VMEM] * len(operands),
        out_specs=(VMEM,) * len(shapes),
        compiler_params=SMALL,
        cost_estimate=SOON,
        name=name,
    )(*operands)


DOT = object()


def finish_kernel(segments, count, *refs):
    out = refs[count]
    for left in range(0, out.shape[1], 128):
        rows_of = []
        for _, _, rows, terms in segments:
            value = None
            for operand, place, first in terms:
                term = refs[operand][place, first : first + rows, left : left + 128]
                value = term if value is None else value + term
            rows_of.append(value)
        value = jnp.concatenate(rows_of, axis=0) if len(rows_of) > 1 else rows_of[0]
        out[0, left : left + 128, :] = value.T.astype(out.dtype)


def finish(segments, head, width):
    if width % 128:
        (value,) = plain_blocks(None, None, width, [segments])
        return value.swapaxes(1, 2).astype(jnp.bfloat16)
    operands = []
    (static,) = number_operands([segments], operands)
    return pl.pallas_call(
        functools.partial(finish_kernel, static, len(operands)),
        out_shape=jax.ShapeDtypeStruct((1, width, head), jnp.bfloat16),
        in_specs=[VMEM] * len(operands),
        out_specs=VMEM,
        compiler_params=SMALL,
        cost_estimate=SOON,
        name="finish",
    )(*operands)


class Section:
    def __init__(self, half, chips):
        self.half = half
        self.dots = [True] * chips
        self.given = [[] for _ in range(chips)]

    def add(self, block, low, high, array, slab=0):
        self.given[block].append((low, high, array, slab, low))

    def settle(self, block, low, high, array, slab=0):
        kept = []
        for first, last, other, place, top in self.given[block]:
            for start, stop in ((first, min(last, low)), (max(first, high), last)):
                if start < stop:
                    kept.append((start, stop, other, place, top))
        self.given[block] = kept
        self.add(block, low, high, array, slab)

    def segments(self, block, low, high, slab=0):
        edges = {low, high}
        for start, stop, *_ in self.given[block]:
            edges |= {start, stop}
        edges = sorted(edge for edge in edges if low <= edge <= high)
        made = []
        for start, stop in zip(edges, edges[1:]):
            terms = [(DOT, self.half, 2 * block, start)] if self.dots[block] else []
            terms += [
                (array, place, start - top)
                for first, last, array, place, top in self.given[block]
                if first <= start and stop <= last
            ]
            made.append((slab, start - low, stop - start, terms))
        return made


def order(chips, head):
    last = chips - 1
    half = head // 2
    everything = list(reversed(range(chips)))
    pairs = [(1, block) for block in everything[1:]] + [(0, block) for block in everything[1:]]
    if chips < 4:
        events = [("core", *pairs)] if pairs else []
        events += [("up", block, 0, head) for block in everything] + [("base", *everything)]
        return events + [("down", block, 0, head) for block in everything[:-1]]
    events = [
        ("core", *pairs),
        ("up", last, 0, half),
        ("raw", last, half, head),
        ("up", last - 1, 0, half),
        ("up", 1, 0, half),
        ("base", *everything),
        ("down", last, 0, half),
        ("up", last - 1, half, head),
    ]
    for block in reversed(range(2, last - 1)):
        events += [("up", block, 0, head), ("down", block + 1, 0, head)]
    parts = [(0, half), (half, head)] if last - 1 == 2 else [(0, head)]
    events += [("down", 2, *parts[0]), ("down", 1, 0, half), ("up", 1, half, head)]
    events += [("down", 2, *part) for part in parts[1:]]
    events += [("up", 0, 0, head), ("down", 1, half, head)]
    return events + [("take", 0, *part, "down2") for part in parts]


def body(activations, queries, keys, grad_out, segment_ids):
    ways = lax.axis_size("dp")
    slots = lax.axis_size("pipe")
    chips = ways // 2
    head = queries.shape[3]
    width = activations.shape[3] // ways
    last = chips - 1

    def swap(block, distance):
        return lax.ppermute(block, "dp", [(i, i ^ distance) for i in range(ways)])

    def mirror(block):
        return lax.ppermute(block, "pipe", [(i, slots - 1 - i) for i in range(slots)])

    grads, first = front(
        activations, queries, keys, grad_out, segment_ids, 2 * last + 1, width
    )
    lower, upper = Section(0, chips), Section(1, chips)
    got = swap(first, 1)
    for section in (upper, lower):
        section.add(last, 0, head, got, 1 - section.half)
    token = None

    def make(name, plan):
        nonlocal token
        *made, token = blocks(name, activations, grads, width, plan, token)
        return made

    def exchange(wanted):
        plan = [
            (slab, 0, head, [(DOT, section.half, 2 * block + 1, 0)])
            for slab, (section, block) in enumerate(wanted)
        ]
        got = swap(make("theirs", [plan])[0], 1)
        for slab, (section, block) in enumerate(wanted):
            section.add(block, 0, head, got, slab)

    def send_up(block, low, high):
        (part,) = make("upper", [upper.segments(block, low, high)])
        return mirror(part)

    def send_raw(block, low, high):
        rows = (block, low, high)
        (both,) = make("raw", [upper.segments(*rows, 0) + lower.segments(*rows, 1)])
        bit = block & -block
        got = swap(both, 2 * bit)
        upper.add(block ^ bit, low, high, got, 0)
        late.append((block ^ bit, low, high, got, 1, "raw"))

    def send_down(block, low, high):
        (part,) = make("lower", [lower.segments(block, low, high)])
        bit = block & -block
        late.append((block ^ bit, low, high, swap(part, 2 * bit), 0, f"down{block}"))

    def settle(blocks_of):
        sums = make("base", [lower.segments(block, 0, head) for block in blocks_of])
        for block, array in zip(blocks_of, sums):
            lower.dots[block] = False
            lower.settle(block, 0, head, array)

    def take(block, low, high):
        (part,) = make("take", [lower.segments(block, low, high)])
        lower.settle(block, low, high, part)

    late = []

    def arrive(block, low, high, kind=None):
        waiting = late[:]
        late.clear()
        for entry in waiting:
            inside = entry[0] == block and low <= entry[1] and entry[2] <= high
            if inside and kind in (None, entry[5]):
                lower.add(*entry[:5])
            else:
                late.append(entry)

    for event, *what in order(chips, head):
        if event == "core":
            exchange([(upper if half else lower, block) for half, block in what])
        elif event == "base":
            settle(what)
        elif event == "up":
            late.append((*what, send_up(*what), 0, "up"))
        elif event == "raw":
            send_raw(*what)
        elif event == "down":
            arrive(*what)
            send_down(*what)
        elif event == "take":
            arrive(*what)
            take(*what[:3])
    arrive(0, 0, head)
    assert not late
    return finish(lower.segments(0, 0, head), head, width)


def solution(mesh):
    spec = P(None, "pipe", "dp", None)
    return jax.shard_map(
        body,
        mesh=mesh,
        in_specs=(spec,) * 5,
        out_specs=P("pipe", "dp", None),
        check_vma=False,
    )
```

```python
import functools

import jax
import jax.numpy as jnp
from jax import lax
from jax.experimental import pallas as pl
from jax.experimental.pallas import tpu as pltpu
from jax.sharding import PartitionSpec as P

VMEM = pl.BlockSpec(memory_space=pltpu.VMEM)
SOON = pl.CostEstimate(flops=10_000_000_000, bytes_accessed=1000, transcendentals=0)
SMALL = pltpu.CompilerParams(vmem_limit_bytes=8 << 20)


def grad_v_columns(query_rows, key_rows, grad_rows, segs):
    length, head = query_rows[0].shape
    count = len(query_rows)
    scores = [
        lax.dot_general(q, k, (((1,), (1,)), ((), ())), preferred_element_type=jnp.float32)
        for q, k in zip(query_rows, key_rows)
    ]
    scores = jnp.concatenate(scores, axis=0) / jnp.sqrt(jnp.float32(head))
    square = (length, length)
    across = [jnp.broadcast_to(row, square) for row in segs]
    same = jnp.concatenate(across, axis=0) == jnp.concatenate([x.T for x in across], axis=0)
    before = lax.broadcasted_iota(jnp.int32, square, 1) <= lax.broadcasted_iota(
        jnp.int32, square, 0
    )
    keep = same & jnp.concatenate([before] * count, axis=0)
    masked = jnp.where(keep, scores, jnp.float32(-1e30))
    top = jnp.max(masked, axis=1, keepdims=True)
    weights = jnp.where(keep, jnp.exp(masked - top), jnp.float32(0.0))
    probs = (weights / jnp.sum(weights, axis=1, keepdims=True)).astype(jnp.bfloat16)
    return [
        lax.dot_general(
            grad,
            probs[i * length : (i + 1) * length],
            (((0,), (0,)), ((), ())),
            preferred_element_type=jnp.float32,
        ).astype(jnp.bfloat16)
        for i, grad in enumerate(grad_rows)
    ]


def block_columns(flip, width):
    owner = lax.axis_index("dp") ^ flip
    return pl.ds(pl.multiple_of(owner * width, 128), width)


def front_kernel(flip, width, acts, queries, keys, grad_out, segs, grads, first, *scratch):
    columns, ready = scratch[0], scratch[-1]
    sources = [queries, keys, grad_out, segs, acts.at[:, 0, :, block_columns(flip, width)]]
    holders = [*scratch[1:-1], columns]
    copies = [
        pltpu.make_async_copy(source, holder, ready.at[i])
        for i, (source, holder) in enumerate(zip(sources, holders))
    ]
    for copy in copies:
        copy.start()
    for copy in copies[:-1]:
        copy.wait()
    made = grad_v_columns(*([holder[half, 0] for half in range(2)] for holder in scratch[1:-1]))
    for half in range(2):
        grads[half] = made[half]
    copies[-1].wait()
    for slab in range(2):
        first[slab] = jnp.dot(made[1 - slab], columns[1 - slab], preferred_element_type=jnp.float32)


def front(activations, queries, keys, grad_out, segment_ids, flip, width):
    head, length = queries.shape[3], queries.shape[2]
    if width % 128:
        small = (queries, keys, grad_out, segment_ids)
        grads = jnp.stack(grad_v_columns(*([x[half, 0] for half in range(2)] for x in small)))
        return grads, *plain_blocks(
            activations,
            grads,
            width,
            [[(slab, 0, head, [(DOT, 1 - slab, flip, 0)]) for slab in range(2)]],
        )
    small = (queries, keys, grad_out, segment_ids)
    return pl.pallas_call(
        functools.partial(front_kernel, flip, width),
        out_shape=(
            jax.ShapeDtypeStruct((2, head, length), jnp.bfloat16),
            jax.ShapeDtypeStruct((2, head, width), jnp.float32),
        ),
        in_specs=[pl.BlockSpec(memory_space=pltpu.HBM)] * 5,
        out_specs=(VMEM, VMEM),
        scratch_shapes=[
            pltpu.VMEM((2, length, width), activations.dtype),
            *(pltpu.VMEM(value.shape, value.dtype) for value in small),
            pltpu.SemaphoreType.DMA((5,)),
        ],
        compiler_params=SMALL,
        cost_estimate=SOON,
        name="front",
    )(*(pltpu.with_memory_space_constraint(x, pltpu.HBM) for x in (activations, *small)))


def extent(segments):
    slabs = max(slab for slab, _, _, _ in segments) + 1
    return slabs, max(low + rows for _, low, rows, _ in segments)


def plain_blocks(acts, grads, width, plan):
    outs = []
    for segments in plan:
        out = jnp.zeros((*extent(segments), width), jnp.float32)
        for slab, low, rows, terms in segments:
            value = None
            for term in terms:
                if term[0] is DOT:
                    _, half, flip, head_low = term
                    owner = lax.axis_index("dp") ^ flip
                    columns = lax.dynamic_slice_in_dim(acts[half, 0], owner * width, width, axis=1)
                    term = jnp.dot(
                        grads[half, head_low : head_low + rows],
                        columns,
                        preferred_element_type=jnp.float32,
                    )
                else:
                    array, place, first = term
                    term = array[place, first : first + rows]
                value = term if value is None else value + term
            out = out.at[slab, low : low + rows].set(value)
        outs.append(out)
    return tuple(outs)


def blocks_kernel(plan, count, width, *refs):
    acts, grads = refs[0], refs[1]
    refs[-1][...] = jnp.zeros_like(refs[-1])
    for out, segments in zip(refs[count:-1], plan):
        for slab, low, rows, terms in segments:
            value = None
            for term in terms:
                if term[0] is DOT:
                    _, half, flip, head_low = term
                    term = jnp.dot(
                        grads[half, head_low : head_low + rows, :],
                        acts[half, 0, :, block_columns(flip, width)],
                        preferred_element_type=jnp.float32,
                    )
                else:
                    operand, place, first = term
                    term = refs[operand][place, first : first + rows, :]
                value = term if value is None else value + term
            out[slab, low : low + rows, :] = value


def number_operands(plan, operands):
    numbers = {}

    def numbered(term):
        if term[0] is DOT:
            return term
        if id(term[0]) not in numbers:
            numbers[id(term[0])] = len(operands)
            operands.append(term[0])
        return (numbers[id(term[0])], *term[1:])

    return [
        [(slab, low, rows, [numbered(term) for term in terms]) for slab, low, rows, terms in segments]
        for segments in plan
    ]


def blocks(name, acts, grads, width, plan, token):
    if width % 128:
        return *plain_blocks(acts, grads, width, plan), None
    operands = [acts, grads]
    static = number_operands(plan, operands)
    if token is not None:
        operands.append(token)
    shapes = [(*extent(segments), width) for segments in static] + [(8, 128)]
    return pl.pallas_call(
        functools.partial(blocks_kernel, static, len(operands), width),
        out_shape=tuple(jax.ShapeDtypeStruct(shape, jnp.float32) for shape in shapes),
        in_specs=[VMEM] * len(operands),
        out_specs=(VMEM,) * len(shapes),
        compiler_params=SMALL,
        cost_estimate=SOON,
        name=name,
    )(*operands)


DOT = object()


def finish_kernel(segments, count, *refs):
    out = refs[count]
    for left in range(0, out.shape[1], 128):
        rows_of = []
        for _, _, rows, terms in segments:
            value = None
            for operand, place, first in terms:
                term = refs[operand][place, first : first + rows, left : left + 128]
                value = term if value is None else value + term
            rows_of.append(value)
        value = jnp.concatenate(rows_of, axis=0) if len(rows_of) > 1 else rows_of[0]
        out[0, left : left + 128, :] = value.T.astype(out.dtype)


def finish(segments, head, width, token):
    if width % 128:
        (value,) = plain_blocks(None, None, width, [segments])
        return value.swapaxes(1, 2).astype(jnp.bfloat16)
    operands = []
    (static,) = number_operands([segments], operands)
    operands.append(token)
    return pl.pallas_call(
        functools.partial(finish_kernel, static, len(operands)),
        out_shape=jax.ShapeDtypeStruct((1, width, head), jnp.bfloat16),
        in_specs=[VMEM] * len(operands),
        out_specs=VMEM,
        compiler_params=SMALL,
        cost_estimate=SOON,
        name="finish",
    )(*operands)


class Section:
    def __init__(self, half, chips):
        self.half = half
        self.dots = [True] * chips
        self.given = [[] for _ in range(chips)]

    def add(self, block, low, high, array, slab=0):
        self.given[block].append((low, high, array, slab, low))

    def settle(self, block, low, high, array, slab=0):
        kept = []
        for first, last, other, place, top in self.given[block]:
            for start, stop in ((first, min(last, low)), (max(first, high), last)):
                if start < stop:
                    kept.append((start, stop, other, place, top))
        self.given[block] = kept
        self.add(block, low, high, array, slab)

    def segments(self, block, low, high, slab=0):
        edges = {low, high}
        for start, stop, *_ in self.given[block]:
            edges |= {start, stop}
        edges = sorted(edge for edge in edges if low <= edge <= high)
        made = []
        for start, stop in zip(edges, edges[1:]):
            terms = [(DOT, self.half, 2 * block, start)] if self.dots[block] else []
            terms += [
                (array, place, start - top)
                for first, last, array, place, top in self.given[block]
                if first <= start and stop <= last
            ]
            made.append((slab, start - low, stop - start, terms))
        return made


def order(chips, head):
    last = chips - 1
    half = head // 2
    everything = list(reversed(range(chips)))
    pairs = [(1, block) for block in everything[1:]] + [(0, block) for block in everything[1:]]
    if chips < 4:
        events = [("core", *pairs)] if pairs else []
        events += [("up", (block, 0, head)) for block in everything] + [("base", *everything)]
        return events + [("down", (block, 0, head)) for block in everything[:-1]]
    events = [
        ("core", *pairs),
        ("up", (last, 0, half)),
        ("raw upper", last, half, head),
        ("up", (last - 1, 0, half), (1, 0, half)),
        ("base", *everything),
        ("down", (last, 0, half)),
        ("raw lower", last, half, head),
        ("up", (last - 1, half, head), (1, half, head)),
    ]
    for block in reversed(range(2, last - 1)):
        events += [("up", (block, 0, head)), ("down", (block + 1, 0, head))]
    parts = [(0, half), (half, head)] if last - 1 == 2 else [(0, head)]
    events += [("down", (2, *parts[0])), ("down", (1, 0, half)), ("up", (0, 0, head))]
    events += [("down", (2, *part)) for part in parts[1:]]
    return events + [("down", (1, half, head))]


def body(activations, queries, keys, grad_out, segment_ids):
    ways = lax.axis_size("dp")
    slots = lax.axis_size("pipe")
    chips = ways // 2
    head = queries.shape[3]
    width = activations.shape[3] // ways
    last = chips - 1

    def swap(block, distance):
        return lax.ppermute(block, "dp", [(i, i ^ distance) for i in range(ways)])

    def mirror(block):
        return lax.ppermute(block, "pipe", [(i, slots - 1 - i) for i in range(slots)])

    grads, first = front(
        activations, queries, keys, grad_out, segment_ids, 2 * last + 1, width
    )
    lower, upper = Section(0, chips), Section(1, chips)
    got = swap(first, 1)
    for section in (upper, lower):
        section.add(last, 0, head, got, 1 - section.half)
    token = None

    def make(name, plan):
        nonlocal token
        *made, token = blocks(name, activations, grads, width, plan, token)
        return made

    def exchange(wanted):
        plan = [
            (slab, 0, head, [(DOT, section.half, 2 * block + 1, 0)])
            for slab, (section, block) in enumerate(wanted)
        ]
        got = swap(make("theirs", [plan])[0], 1)
        for slab, (section, block) in enumerate(wanted):
            section.add(block, 0, head, got, slab)

    def send_up(*wanted):
        plan = []
        for slab, rows in enumerate(wanted):
            plan += upper.segments(*rows, slab)
        (part,) = make("upper", [plan])
        got = mirror(part)
        for slab, rows in enumerate(wanted):
            late.append((*rows, got, slab))

    def send_raw(name, block, low, high):
        bit = block & -block
        sections = {"raw": (upper, lower), "raw upper": (upper,), "raw lower": (lower,)}[name]
        plan = []
        for slab, section in enumerate(sections):
            plan += section.segments(block, low, high, slab)
        got = swap(make("raw", [plan])[0], 2 * bit)
        for slab, section in enumerate(sections):
            if section is upper:
                upper.add(block ^ bit, low, high, got, slab)
            else:
                late.append((block ^ bit, low, high, got, slab))

    def send_down(*wanted):
        bit = wanted[0][0] & -wanted[0][0]
        plan = []
        for slab, rows in enumerate(wanted):
            arrive(*rows)
            plan += lower.segments(*rows, slab)
        (part,) = make("lower", [plan])
        got = swap(part, 2 * bit)
        for slab, (block, low, high) in enumerate(wanted):
            late.append((block ^ bit, low, high, got, slab))

    def settle(blocks_of):
        sums = make("base", [lower.segments(block, 0, head) for block in blocks_of])
        for block, array in zip(blocks_of, sums):
            lower.dots[block] = False
            lower.settle(block, 0, head, array)

    late = []

    def arrive(block, low, high):
        waiting = late[:]
        late.clear()
        for entry in waiting:
            if entry[0] == block and low <= entry[1] and entry[2] <= high:
                lower.add(*entry)
            else:
                late.append(entry)

    for event, *what in order(chips, head):
        if event == "core":
            exchange([(upper if half else lower, block) for half, block in what])
        elif event == "base":
            settle(what)
        elif event == "up":
            send_up(*what)
        elif event.startswith("raw"):
            send_raw(event, *what)
        elif event == "down":
            send_down(*what)
    arrive(0, 0, head)
    assert not late
    return finish(lower.segments(0, 0, head), head, width, token)


def solution(mesh):
    spec = P(None, "pipe", "dp", None)
    return jax.shard_map(
        body,
        mesh=mesh,
        in_specs=(spec,) * 5,
        out_specs=P("pipe", "dp", None),
        check_vma=False,
    )
```

```python
import functools

import jax
import jax.numpy as jnp
from jax import lax
from jax.experimental import pallas as pl
from jax.experimental.pallas import tpu as pltpu
from jax.sharding import PartitionSpec as P

VMEM = pl.BlockSpec(memory_space=pltpu.VMEM)
SOON = pl.CostEstimate(flops=25_000_000_000, bytes_accessed=1000, transcendentals=0)
SMALL = pltpu.CompilerParams(vmem_limit_bytes=8 << 20)


def grad_v_columns(query_rows, key_rows, grad_rows, segs):
    length, head = query_rows[0].shape
    count = len(query_rows)
    scores = [
        lax.dot_general(q, k, (((1,), (1,)), ((), ())), preferred_element_type=jnp.float32)
        for q, k in zip(query_rows, key_rows)
    ]
    scores = jnp.concatenate(scores, axis=0) / jnp.sqrt(jnp.float32(head))
    square = (length, length)
    across = [jnp.broadcast_to(row, square) for row in segs]
    same = jnp.concatenate(across, axis=0) == jnp.concatenate([x.T for x in across], axis=0)
    before = lax.broadcasted_iota(jnp.int32, square, 1) <= lax.broadcasted_iota(
        jnp.int32, square, 0
    )
    keep = same & jnp.concatenate([before] * count, axis=0)
    masked = jnp.where(keep, scores, jnp.float32(-1e30))
    top = jnp.max(masked, axis=1, keepdims=True)
    weights = jnp.where(keep, jnp.exp(masked - top), jnp.float32(0.0))
    probs = (weights / jnp.sum(weights, axis=1, keepdims=True)).astype(jnp.bfloat16)
    return [
        lax.dot_general(
            grad,
            probs[i * length : (i + 1) * length],
            (((0,), (0,)), ((), ())),
            preferred_element_type=jnp.float32,
        ).astype(jnp.bfloat16)
        for i, grad in enumerate(grad_rows)
    ]


def block_columns(flip, width):
    owner = lax.axis_index("dp") ^ flip
    return pl.ds(pl.multiple_of(owner * width, 128), width)


def front_kernel(flip, width, acts, queries, keys, grad_out, segs, grads, first, *scratch):
    columns, ready = scratch[0], scratch[-1]
    sources = [queries, keys, grad_out, segs, acts.at[1, 0, :, block_columns(flip, width)]]
    holders = [*scratch[1:-1], columns]
    copies = [
        pltpu.make_async_copy(source, holder, ready.at[i])
        for i, (source, holder) in enumerate(zip(sources, holders))
    ]
    for copy in copies:
        copy.start()
    for copy in copies[:-1]:
        copy.wait()
    made = grad_v_columns(*([holder[half, 0] for half in range(2)] for holder in scratch[1:-1]))
    for half in range(2):
        grads[half] = made[half]
    copies[-1].wait()
    first[0] = jnp.dot(made[1], columns[...], preferred_element_type=jnp.float32)


def front(activations, queries, keys, grad_out, segment_ids, flip, width):
    head, length = queries.shape[3], queries.shape[2]
    if width % 128:
        small = (queries, keys, grad_out, segment_ids)
        grads = jnp.stack(grad_v_columns(*([x[half, 0] for half in range(2)] for x in small)))
        plan = [[(0, 0, head, [(DOT, 1, flip, 0)])]]
        return grads, *plain_blocks(activations, grads, width, plan)
    small = (queries, keys, grad_out, segment_ids)
    return pl.pallas_call(
        functools.partial(front_kernel, flip, width),
        out_shape=(
            jax.ShapeDtypeStruct((2, head, length), jnp.bfloat16),
            jax.ShapeDtypeStruct((1, head, width), jnp.float32),
        ),
        in_specs=[pl.BlockSpec(memory_space=pltpu.HBM)] * 5,
        out_specs=(VMEM, VMEM),
        scratch_shapes=[
            pltpu.VMEM((length, width), activations.dtype),
            *(pltpu.VMEM(value.shape, value.dtype) for value in small),
            pltpu.SemaphoreType.DMA((5,)),
        ],
        compiler_params=SMALL,
        cost_estimate=SOON,
        name="front",
    )(*(pltpu.with_memory_space_constraint(x, pltpu.HBM) for x in (activations, *small)))


def extent(segments):
    slabs = max(slab for slab, _, _, _ in segments) + 1
    return slabs, max(low + rows for _, low, rows, _ in segments)


def plain_blocks(acts, grads, width, plan):
    outs = []
    for segments in plan:
        out = jnp.zeros((*extent(segments), width), jnp.float32)
        for slab, low, rows, terms in segments:
            value = None
            for term in terms:
                if term[0] is DOT:
                    _, half, flip, head_low = term
                    owner = lax.axis_index("dp") ^ flip
                    columns = lax.dynamic_slice_in_dim(acts[half, 0], owner * width, width, axis=1)
                    term = jnp.dot(
                        grads[half, head_low : head_low + rows],
                        columns,
                        preferred_element_type=jnp.float32,
                    )
                else:
                    array, place, first = term
                    term = array[place, first : first + rows]
                value = term if value is None else value + term
            out = out.at[slab, low : low + rows].set(value)
        outs.append(out)
    return tuple(outs)


def blocks_kernel(plan, count, width, *refs):
    acts, grads = refs[0], refs[1]
    refs[-1][...] = jnp.zeros_like(refs[-1])
    for out, segments in zip(refs[count:-1], plan):
        for slab, low, rows, terms in segments:
            value = None
            for term in terms:
                if term[0] is DOT:
                    _, half, flip, head_low = term
                    term = jnp.dot(
                        grads[half, head_low : head_low + rows, :],
                        acts[half, 0, :, block_columns(flip, width)],
                        preferred_element_type=jnp.float32,
                    )
                else:
                    operand, place, first = term
                    term = refs[operand][place, first : first + rows, :]
                value = term if value is None else value + term
            out[slab, low : low + rows, :] = value


def number_operands(plan, operands):
    numbers = {}

    def numbered(term):
        if term[0] is DOT:
            return term
        if id(term[0]) not in numbers:
            numbers[id(term[0])] = len(operands)
            operands.append(term[0])
        return (numbers[id(term[0])], *term[1:])

    return [
        [(slab, low, rows, [numbered(term) for term in terms]) for slab, low, rows, terms in segments]
        for segments in plan
    ]


def blocks(name, acts, grads, width, plan, token):
    if width % 128:
        return *plain_blocks(acts, grads, width, plan), None
    operands = [acts, grads]
    static = number_operands(plan, operands)
    if token is not None:
        operands.append(token)
    shapes = [(*extent(segments), width) for segments in static] + [(8, 128)]
    return pl.pallas_call(
        functools.partial(blocks_kernel, static, len(operands), width),
        out_shape=tuple(jax.ShapeDtypeStruct(shape, jnp.float32) for shape in shapes),
        in_specs=[VMEM] * len(operands),
        out_specs=(VMEM,) * len(shapes),
        compiler_params=SMALL,
        cost_estimate=SOON,
        name=name,
    )(*operands)


DOT = object()


def finish_kernel(segments, count, *refs):
    out = refs[count]
    for left in range(0, out.shape[1], 128):
        rows_of = []
        for _, _, rows, terms in segments:
            value = None
            for operand, place, first in terms:
                term = refs[operand][place, first : first + rows, left : left + 128]
                value = term if value is None else value + term
            rows_of.append(value)
        value = jnp.concatenate(rows_of, axis=0) if len(rows_of) > 1 else rows_of[0]
        out[0, left : left + 128, :] = value.T.astype(out.dtype)


def finish(segments, head, width, token):
    if width % 128:
        (value,) = plain_blocks(None, None, width, [segments])
        return value.swapaxes(1, 2).astype(jnp.bfloat16)
    operands = []
    (static,) = number_operands([segments], operands)
    operands.append(token)
    return pl.pallas_call(
        functools.partial(finish_kernel, static, len(operands)),
        out_shape=jax.ShapeDtypeStruct((1, width, head), jnp.bfloat16),
        in_specs=[VMEM] * len(operands),
        out_specs=VMEM,
        compiler_params=SMALL,
        cost_estimate=SOON,
        name="finish",
    )(*operands)


class Section:
    def __init__(self, half, chips):
        self.half = half
        self.dots = [True] * chips
        self.given = [[] for _ in range(chips)]

    def add(self, block, low, high, array, slab=0):
        self.given[block].append((low, high, array, slab, low))

    def settle(self, block, low, high, array, slab=0):
        kept = []
        for first, last, other, place, top in self.given[block]:
            for start, stop in ((first, min(last, low)), (max(first, high), last)):
                if start < stop:
                    kept.append((start, stop, other, place, top))
        self.given[block] = kept
        self.add(block, low, high, array, slab)

    def segments(self, block, low, high, slab=0):
        edges = {low, high}
        for start, stop, *_ in self.given[block]:
            edges |= {start, stop}
        edges = sorted(edge for edge in edges if low <= edge <= high)
        made = []
        for start, stop in zip(edges, edges[1:]):
            terms = [(DOT, self.half, 2 * block, start)] if self.dots[block] else []
            terms += [
                (array, place, start - top)
                for first, last, array, place, top in self.given[block]
                if first <= start and stop <= last
            ]
            made.append((slab, start - low, stop - start, terms))
        return made


def order(chips, head):
    last = chips - 1
    half = head // 2
    everything = list(reversed(range(chips)))
    pairs = [(1, block) for block in everything[1:]] + [(0, block) for block in everything]
    if chips < 4:
        events = [("core", *pairs)]
        events += [("up", (block, 0, head)) for block in everything] + [("base", *everything)]
        return events + [("down", (block, 0, head)) for block in everything[:-1]]
    events = [
        ("core", *pairs),
        ("up", (last, 0, half)),
        ("raw upper", last, half, head),
        ("up", (last - 1, 0, half), (1, 0, half)),
        ("base", *everything),
        ("down", (last, 0, half)),
        ("raw lower", last, half, head),
        ("up", (last - 1, half, head), (1, half, head)),
    ]
    for block in reversed(range(2, last - 1)):
        events += [("up", (block, 0, head)), ("down", (block + 1, 0, head))]
    parts = [(0, half), (half, head)] if last - 1 == 2 else [(0, head)]
    events += [("down", (2, *parts[0])), ("down", (1, 0, half)), ("up", (0, 0, head))]
    events += [("down", (2, *part)) for part in parts[1:]]
    return events + [("down", (1, half, head))]


def body(activations, queries, keys, grad_out, segment_ids):
    ways = lax.axis_size("dp")
    slots = lax.axis_size("pipe")
    chips = ways // 2
    head = queries.shape[3]
    width = activations.shape[3] // ways
    last = chips - 1

    def swap(block, distance):
        return lax.ppermute(block, "dp", [(i, i ^ distance) for i in range(ways)])

    def mirror(block):
        return lax.ppermute(block, "pipe", [(i, slots - 1 - i) for i in range(slots)])

    grads, first = front(
        activations, queries, keys, grad_out, segment_ids, 2 * last + 1, width
    )
    lower, upper = Section(0, chips), Section(1, chips)
    upper.add(last, 0, head, swap(first, 1))
    token = None

    def make(name, plan):
        nonlocal token
        *made, token = blocks(name, activations, grads, width, plan, token)
        return made

    def exchange(wanted):
        plan = [
            (slab, 0, head, [(DOT, section.half, 2 * block + 1, 0)])
            for slab, (section, block) in enumerate(wanted)
        ]
        got = swap(make("theirs", [plan])[0], 1)
        for slab, (section, block) in enumerate(wanted):
            section.add(block, 0, head, got, slab)

    def send_up(*wanted):
        plan = []
        for slab, rows in enumerate(wanted):
            plan += upper.segments(*rows, slab)
        (part,) = make("upper", [plan])
        got = mirror(part)
        for slab, rows in enumerate(wanted):
            late.append((*rows, got, slab))

    def send_raw(name, block, low, high):
        bit = block & -block
        sections = {"raw": (upper, lower), "raw upper": (upper,), "raw lower": (lower,)}[name]
        plan = []
        for slab, section in enumerate(sections):
            plan += section.segments(block, low, high, slab)
        got = swap(make("raw", [plan])[0], 2 * bit)
        for slab, section in enumerate(sections):
            if section is upper:
                upper.add(block ^ bit, low, high, got, slab)
            else:
                late.append((block ^ bit, low, high, got, slab))

    def send_down(*wanted):
        bit = wanted[0][0] & -wanted[0][0]
        plan = []
        for slab, rows in enumerate(wanted):
            arrive(*rows)
            plan += lower.segments(*rows, slab)
        (part,) = make("lower", [plan])
        got = swap(part, 2 * bit)
        for slab, (block, low, high) in enumerate(wanted):
            late.append((block ^ bit, low, high, got, slab))

    def settle(blocks_of):
        sums = make("base", [lower.segments(block, 0, head) for block in blocks_of])
        for block, array in zip(blocks_of, sums):
            lower.dots[block] = False
            lower.settle(block, 0, head, array)

    late = []

    def arrive(block, low, high):
        waiting = late[:]
        late.clear()
        for entry in waiting:
            if entry[0] == block and low <= entry[1] and entry[2] <= high:
                lower.add(*entry)
            else:
                late.append(entry)

    for event, *what in order(chips, head):
        if event == "core":
            exchange([(upper if half else lower, block) for half, block in what])
        elif event == "base":
            settle(what)
        elif event == "up":
            send_up(*what)
        elif event.startswith("raw"):
            send_raw(event, *what)
        elif event == "down":
            send_down(*what)
    arrive(0, 0, head)
    assert not late
    return finish(lower.segments(0, 0, head), head, width, token)


def solution(mesh):
    spec = P(None, "pipe", "dp", None)
    return jax.shard_map(
        body,
        mesh=mesh,
        in_specs=(spec,) * 5,
        out_specs=P("pipe", "dp", None),
        check_vma=False,
    )
```

```python
import functools

import jax
import jax.numpy as jnp
from jax import lax
from jax.experimental import pallas as pl
from jax.experimental.pallas import tpu as pltpu
from jax.sharding import PartitionSpec as P

VMEM = pl.BlockSpec(memory_space=pltpu.VMEM)
SOON = pl.CostEstimate(flops=25_000_000_000, bytes_accessed=1000, transcendentals=0)
SMALL = pltpu.CompilerParams(vmem_limit_bytes=8 << 20)


def grad_v_columns(query_rows, key_rows, grad_rows, segs):
    length, head = query_rows[0].shape
    count = len(query_rows)
    scores = [
        lax.dot_general(k, q, (((1,), (1,)), ((), ())), preferred_element_type=jnp.float32)
        for q, k in zip(query_rows, key_rows)
    ]
    scores = jnp.concatenate(scores, axis=1) / jnp.sqrt(jnp.float32(head))
    square = (length, length)
    across = [jnp.broadcast_to(row, square) for row in segs]
    same = jnp.concatenate(across, axis=1) == jnp.concatenate([x.T for x in across], axis=1)
    before = lax.broadcasted_iota(jnp.int32, square, 0) <= lax.broadcasted_iota(
        jnp.int32, square, 1
    )
    keep = same & jnp.concatenate([before] * count, axis=1)
    masked = jnp.where(keep, scores, jnp.float32(-1e30))
    top = jnp.max(masked, axis=0, keepdims=True)
    weights = jnp.where(keep, jnp.exp(masked - top), jnp.float32(0.0))
    probs = (weights / jnp.sum(weights, axis=0, keepdims=True)).astype(jnp.bfloat16)
    return [
        lax.dot_general(
            grad.astype(jnp.float32).T.astype(jnp.bfloat16),
            probs[:, i * length : (i + 1) * length],
            (((1,), (1,)), ((), ())),
            preferred_element_type=jnp.float32,
        ).astype(jnp.bfloat16)
        for i, grad in enumerate(grad_rows)
    ]


def block_columns(flip, width):
    owner = lax.axis_index("dp") ^ flip
    return pl.ds(pl.multiple_of(owner * width, 128), width)


def front_kernel(flip, width, acts, queries, keys, grad_out, segs, grads, first, *scratch):
    columns, ready = scratch[0], scratch[-1]
    sources = [queries, keys, grad_out, segs, acts.at[1, 0, :, block_columns(flip, width)]]
    holders = [*scratch[1:-1], columns]
    copies = [
        pltpu.make_async_copy(source, holder, ready.at[i])
        for i, (source, holder) in enumerate(zip(sources, holders))
    ]
    for copy in copies:
        copy.start()
    for copy in copies[:-1]:
        copy.wait()
    made = grad_v_columns(*([holder[half, 0] for half in range(2)] for holder in scratch[1:-1]))
    for half in range(2):
        grads[half] = made[half]
    copies[-1].wait()
    first[0] = jnp.dot(made[1], columns[...], preferred_element_type=jnp.float32)


def front(activations, queries, keys, grad_out, segment_ids, flip, width):
    head, length = queries.shape[3], queries.shape[2]
    if width % 128:
        small = (queries, keys, grad_out, segment_ids)
        grads = jnp.stack(grad_v_columns(*([x[half, 0] for half in range(2)] for x in small)))
        plan = [[(0, 0, head, [(DOT, 1, flip, 0)])]]
        return grads, *plain_blocks(activations, grads, width, plan)
    small = (queries, keys, grad_out, segment_ids)
    return pl.pallas_call(
        functools.partial(front_kernel, flip, width),
        out_shape=(
            jax.ShapeDtypeStruct((2, head, length), jnp.bfloat16),
            jax.ShapeDtypeStruct((1, head, width), jnp.float32),
        ),
        in_specs=[pl.BlockSpec(memory_space=pltpu.HBM)] * 5,
        out_specs=(VMEM, VMEM),
        scratch_shapes=[
            pltpu.VMEM((length, width), activations.dtype),
            *(pltpu.VMEM(value.shape, value.dtype) for value in small),
            pltpu.SemaphoreType.DMA((5,)),
        ],
        compiler_params=SMALL,
        cost_estimate=SOON,
        name="front",
    )(*(pltpu.with_memory_space_constraint(x, pltpu.HBM) for x in (activations, *small)))


def extent(segments):
    slabs = max(slab for slab, _, _, _ in segments) + 1
    return slabs, max(low + rows for _, low, rows, _ in segments)


def plain_blocks(acts, grads, width, plan):
    outs = []
    for segments in plan:
        out = jnp.zeros((*extent(segments), width), jnp.float32)
        for slab, low, rows, terms in segments:
            value = None
            for term in terms:
                if term[0] is DOT:
                    _, half, flip, head_low = term
                    owner = lax.axis_index("dp") ^ flip
                    columns = lax.dynamic_slice_in_dim(acts[half, 0], owner * width, width, axis=1)
                    term = jnp.dot(
                        grads[half, head_low : head_low + rows],
                        columns,
                        preferred_element_type=jnp.float32,
                    )
                else:
                    array, place, first = term
                    term = array[place, first : first + rows]
                value = term if value is None else value + term
            out = out.at[slab, low : low + rows].set(value)
        outs.append(out)
    return tuple(outs)


def blocks_kernel(plan, count, width, *refs):
    acts, grads = refs[0], refs[1]
    refs[-1][...] = jnp.zeros_like(refs[-1])
    for out, segments in zip(refs[count:-1], plan):
        for slab, low, rows, terms in segments:
            value = None
            for term in terms:
                if term[0] is DOT:
                    _, half, flip, head_low = term
                    term = jnp.dot(
                        grads[half, head_low : head_low + rows, :],
                        acts[half, 0, :, block_columns(flip, width)],
                        preferred_element_type=jnp.float32,
                    )
                else:
                    operand, place, first = term
                    term = refs[operand][place, first : first + rows, :]
                value = term if value is None else value + term
            out[slab, low : low + rows, :] = value


def number_operands(plan, operands):
    numbers = {}

    def numbered(term):
        if term[0] is DOT:
            return term
        if id(term[0]) not in numbers:
            numbers[id(term[0])] = len(operands)
            operands.append(term[0])
        return (numbers[id(term[0])], *term[1:])

    return [
        [(slab, low, rows, [numbered(term) for term in terms]) for slab, low, rows, terms in segments]
        for segments in plan
    ]


def blocks(name, acts, grads, width, plan, token):
    if width % 128:
        return *plain_blocks(acts, grads, width, plan), None
    operands = [acts, grads]
    static = number_operands(plan, operands)
    if token is not None:
        operands.append(token)
    shapes = [(*extent(segments), width) for segments in static] + [(8, 128)]
    return pl.pallas_call(
        functools.partial(blocks_kernel, static, len(operands), width),
        out_shape=tuple(jax.ShapeDtypeStruct(shape, jnp.float32) for shape in shapes),
        in_specs=[VMEM] * len(operands),
        out_specs=(VMEM,) * len(shapes),
        compiler_params=SMALL,
        cost_estimate=SOON,
        name=name,
    )(*operands)


DOT = object()


def finish_kernel(segments, count, *refs):
    out = refs[count]
    for left in range(0, out.shape[1], 128):
        rows_of = []
        for _, _, rows, terms in segments:
            value = None
            for operand, place, first in terms:
                term = refs[operand][place, first : first + rows, left : left + 128]
                value = term if value is None else value + term
            rows_of.append(value)
        value = jnp.concatenate(rows_of, axis=0) if len(rows_of) > 1 else rows_of[0]
        out[0, left : left + 128, :] = value.T.astype(out.dtype)


def finish(segments, head, width, token):
    if width % 128:
        (value,) = plain_blocks(None, None, width, [segments])
        return value.swapaxes(1, 2).astype(jnp.bfloat16)
    operands = []
    (static,) = number_operands([segments], operands)
    operands.append(token)
    return pl.pallas_call(
        functools.partial(finish_kernel, static, len(operands)),
        out_shape=jax.ShapeDtypeStruct((1, width, head), jnp.bfloat16),
        in_specs=[VMEM] * len(operands),
        out_specs=VMEM,
        compiler_params=SMALL,
        cost_estimate=SOON,
        name="finish",
    )(*operands)


class Section:
    def __init__(self, half, chips):
        self.half = half
        self.dots = [True] * chips
        self.given = [[] for _ in range(chips)]

    def add(self, block, low, high, array, slab=0):
        self.given[block].append((low, high, array, slab, low))

    def settle(self, block, low, high, array, slab=0):
        kept = []
        for first, last, other, place, top in self.given[block]:
            for start, stop in ((first, min(last, low)), (max(first, high), last)):
                if start < stop:
                    kept.append((start, stop, other, place, top))
        self.given[block] = kept
        self.add(block, low, high, array, slab)

    def segments(self, block, low, high, slab=0):
        edges = {low, high}
        for start, stop, *_ in self.given[block]:
            edges |= {start, stop}
        edges = sorted(edge for edge in edges if low <= edge <= high)
        made = []
        for start, stop in zip(edges, edges[1:]):
            terms = [(DOT, self.half, 2 * block, start)] if self.dots[block] else []
            terms += [
                (array, place, start - top)
                for first, last, array, place, top in self.given[block]
                if first <= start and stop <= last
            ]
            made.append((slab, start - low, stop - start, terms))
        return made


def order(chips, head):
    last = chips - 1
    half = head // 2
    everything = list(reversed(range(chips)))
    pairs = [(1, block) for block in everything[1:]] + [(0, block) for block in everything]
    if chips < 4:
        events = [("core", *pairs)]
        events += [("up", (block, 0, head)) for block in everything] + [("base", *everything)]
        return events + [("down", (block, 0, head)) for block in everything[:-1]]
    events = [
        ("core", *pairs),
        ("up", (last, 0, half)),
        ("raw upper", last, half, head),
        ("up", (last - 1, 0, half), (1, 0, half)),
        ("base", *everything),
        ("down", (last, 0, half)),
        ("raw lower", last, half, head),
        ("up", (last - 1, half, head), (1, half, head)),
    ]
    for block in reversed(range(2, last - 1)):
        events += [("up", (block, 0, head)), ("down", (block + 1, 0, head))]
    parts = [(0, half), (half, head)] if last - 1 == 2 else [(0, head)]
    events += [("down", (2, *parts[0])), ("down", (1, 0, half)), ("up", (0, 0, head))]
    events += [("down", (2, *part)) for part in parts[1:]]
    return events + [("down", (1, half, head))]


def body(activations, queries, keys, grad_out, segment_ids):
    ways = lax.axis_size("dp")
    slots = lax.axis_size("pipe")
    chips = ways // 2
    head = queries.shape[3]
    width = activations.shape[3] // ways
    last = chips - 1

    def swap(block, distance):
        return lax.ppermute(block, "dp", [(i, i ^ distance) for i in range(ways)])

    def mirror(block):
        return lax.ppermute(block, "pipe", [(i, slots - 1 - i) for i in range(slots)])

    grads, first = front(
        activations, queries, keys, grad_out, segment_ids, 2 * last + 1, width
    )
    lower, upper = Section(0, chips), Section(1, chips)
    upper.add(last, 0, head, swap(first, 1))
    token = None

    def make(name, plan):
        nonlocal token
        *made, token = blocks(name, activations, grads, width, plan, token)
        return made

    def exchange(wanted):
        plan = [
            (slab, 0, head, [(DOT, section.half, 2 * block + 1, 0)])
            for slab, (section, block) in enumerate(wanted)
        ]
        got = swap(make("theirs", [plan])[0], 1)
        for slab, (section, block) in enumerate(wanted):
            section.add(block, 0, head, got, slab)

    def send_up(*wanted):
        plan = []
        for slab, rows in enumerate(wanted):
            plan += upper.segments(*rows, slab)
        (part,) = make("upper", [plan])
        got = mirror(part)
        for slab, rows in enumerate(wanted):
            late.append((*rows, got, slab))

    def send_raw(name, block, low, high):
        bit = block & -block
        sections = {"raw": (upper, lower), "raw upper": (upper,), "raw lower": (lower,)}[name]
        plan = []
        for slab, section in enumerate(sections):
            plan += section.segments(block, low, high, slab)
        got = swap(make("raw", [plan])[0], 2 * bit)
        for slab, section in enumerate(sections):
            if section is upper:
                upper.add(block ^ bit, low, high, got, slab)
            else:
                late.append((block ^ bit, low, high, got, slab))

    def send_down(*wanted):
        bit = wanted[0][0] & -wanted[0][0]
        plan = []
        for slab, rows in enumerate(wanted):
            arrive(*rows)
            plan += lower.segments(*rows, slab)
        (part,) = make("lower", [plan])
        got = swap(part, 2 * bit)
        for slab, (block, low, high) in enumerate(wanted):
            late.append((block ^ bit, low, high, got, slab))

    def settle(blocks_of):
        sums = make("base", [lower.segments(block, 0, head) for block in blocks_of])
        for block, array in zip(blocks_of, sums):
            lower.dots[block] = False
            lower.settle(block, 0, head, array)

    late = []

    def arrive(block, low, high):
        waiting = late[:]
        late.clear()
        for entry in waiting:
            if entry[0] == block and low <= entry[1] and entry[2] <= high:
                lower.add(*entry)
            else:
                late.append(entry)

    for event, *what in order(chips, head):
        if event == "core":
            exchange([(upper if half else lower, block) for half, block in what])
        elif event == "base":
            settle(what)
        elif event == "up":
            send_up(*what)
        elif event.startswith("raw"):
            send_raw(event, *what)
        elif event == "down":
            send_down(*what)
    arrive(0, 0, head)
    assert not late
    return finish(lower.segments(0, 0, head), head, width, token)


def solution(mesh):
    spec = P(None, "pipe", "dp", None)
    return jax.shard_map(
        body,
        mesh=mesh,
        in_specs=(spec,) * 5,
        out_specs=P("pipe", "dp", None),
        check_vma=False,
    )
```

```python
import functools

import jax
import jax.numpy as jnp
from jax import lax
from jax.experimental import pallas as pl
from jax.experimental.pallas import tpu as pltpu
from jax.sharding import PartitionSpec as P

VMEM = pl.BlockSpec(memory_space=pltpu.VMEM)
SOON = pl.CostEstimate(flops=25_000_000_000, bytes_accessed=1000, transcendentals=0)
SMALL = pltpu.CompilerParams(vmem_limit_bytes=8 << 20)


def grad_v_columns(query_rows, key_rows, grad_rows, segs):
    length, head = query_rows[0].shape
    count = len(query_rows)
    scores = [
        lax.dot_general(k, q, (((1,), (1,)), ((), ())), preferred_element_type=jnp.float32)
        for q, k in zip(query_rows, key_rows)
    ]
    scores = jnp.concatenate(scores, axis=1) / jnp.sqrt(jnp.float32(head))
    square = (length, length)
    across = [jnp.broadcast_to(row, square) for row in segs]
    same = jnp.concatenate(across, axis=1) == jnp.concatenate([x.T for x in across], axis=1)
    before = lax.broadcasted_iota(jnp.int32, square, 0) <= lax.broadcasted_iota(
        jnp.int32, square, 1
    )
    keep = same & jnp.concatenate([before] * count, axis=1)
    masked = jnp.where(keep, scores, jnp.float32(-1e30))
    top = jnp.max(masked, axis=0, keepdims=True)
    weights = jnp.where(keep, jnp.exp(masked - top), jnp.float32(0.0))
    probs = (weights / jnp.sum(weights, axis=0, keepdims=True)).astype(jnp.bfloat16)
    return [
        lax.dot_general(
            grad.astype(jnp.float32).T.astype(jnp.bfloat16),
            probs[:, i * length : (i + 1) * length],
            (((1,), (1,)), ((), ())),
            preferred_element_type=jnp.float32,
        ).astype(jnp.bfloat16)
        for i, grad in enumerate(grad_rows)
    ]


def block_columns(flip, width):
    owner = lax.axis_index("dp") ^ flip
    return pl.ds(pl.multiple_of(owner * width, 128), width)


def front_kernel(flip, width, acts, queries, keys, grad_out, segs, grads, first, *scratch):
    columns, ready = scratch[0], scratch[-1]
    sources = [queries, keys, grad_out, segs, acts.at[1, 0, :, block_columns(flip, width)]]
    holders = [*scratch[1:-1], columns]
    copies = [
        pltpu.make_async_copy(source, holder, ready.at[i])
        for i, (source, holder) in enumerate(zip(sources, holders))
    ]
    for copy in copies:
        copy.start()
    for copy in copies[:-1]:
        copy.wait()
    made = grad_v_columns(*([holder[half, 0] for half in range(2)] for holder in scratch[1:-1]))
    for half in range(2):
        grads[half] = made[half]
    copies[-1].wait()
    first[0] = jnp.dot(made[1], columns[...], preferred_element_type=jnp.float32)


def front(activations, queries, keys, grad_out, segment_ids, flip, width):
    head, length = queries.shape[3], queries.shape[2]
    if width % 128:
        small = (queries, keys, grad_out, segment_ids)
        grads = jnp.stack(grad_v_columns(*([x[half, 0] for half in range(2)] for x in small)))
        plan = [[(0, 0, head, [(DOT, 1, flip, 0)])]]
        return grads, *plain_blocks(activations, grads, width, plan)
    small = (queries, keys, grad_out, segment_ids)
    return pl.pallas_call(
        functools.partial(front_kernel, flip, width),
        out_shape=(
            jax.ShapeDtypeStruct((2, head, length), jnp.bfloat16),
            jax.ShapeDtypeStruct((1, head, width), jnp.float32),
        ),
        in_specs=[pl.BlockSpec(memory_space=pltpu.HBM)] * 5,
        out_specs=(VMEM, VMEM),
        scratch_shapes=[
            pltpu.VMEM((length, width), activations.dtype),
            *(pltpu.VMEM(value.shape, value.dtype) for value in small),
            pltpu.SemaphoreType.DMA((5,)),
        ],
        compiler_params=SMALL,
        cost_estimate=SOON,
        name="front",
    )(*(pltpu.with_memory_space_constraint(x, pltpu.HBM) for x in (activations, *small)))


def extent(segments):
    slabs = max(slab for slab, _, _, _ in segments) + 1
    return slabs, max(low + rows for _, low, rows, _ in segments)


def plain_blocks(acts, grads, width, plan):
    outs = []
    for segments in plan:
        out = jnp.zeros((*extent(segments), width), jnp.float32)
        for slab, low, rows, terms in segments:
            value = None
            for term in terms:
                if term[0] is DOT:
                    _, half, flip, head_low = term
                    owner = lax.axis_index("dp") ^ flip
                    columns = lax.dynamic_slice_in_dim(acts[half, 0], owner * width, width, axis=1)
                    term = jnp.dot(
                        grads[half, head_low : head_low + rows],
                        columns,
                        preferred_element_type=jnp.float32,
                    )
                else:
                    array, place, first = term
                    term = array[place, first : first + rows]
                value = term if value is None else value + term
            out = out.at[slab, low : low + rows].set(value)
        outs.append(out)
    return tuple(outs)


def blocks_kernel(plan, count, width, *refs):
    acts, grads = refs[0], refs[1]
    refs[-1][...] = jnp.zeros_like(refs[-1])
    for out, segments in zip(refs[count:-1], plan):
        for slab, low, rows, terms in segments:
            value = None
            for term in terms:
                if term[0] is DOT:
                    _, half, flip, head_low = term
                    term = jnp.dot(
                        grads[half, head_low : head_low + rows, :],
                        acts[half, 0, :, block_columns(flip, width)],
                        preferred_element_type=jnp.float32,
                    )
                else:
                    operand, place, first = term
                    term = refs[operand][place, first : first + rows, :]
                value = term if value is None else value + term
            out[slab, low : low + rows, :] = value


def number_operands(plan, operands):
    numbers = {}

    def numbered(term):
        if term[0] is DOT:
            return term
        if id(term[0]) not in numbers:
            numbers[id(term[0])] = len(operands)
            operands.append(term[0])
        return (numbers[id(term[0])], *term[1:])

    return [
        [(slab, low, rows, [numbered(term) for term in terms]) for slab, low, rows, terms in segments]
        for segments in plan
    ]


def blocks(name, acts, grads, width, plan, token):
    if width % 128:
        return *plain_blocks(acts, grads, width, plan), None
    operands = [acts, grads]
    static = number_operands(plan, operands)
    if token is not None:
        operands.append(token)
    shapes = [(*extent(segments), width) for segments in static] + [(8, 128)]
    return pl.pallas_call(
        functools.partial(blocks_kernel, static, len(operands), width),
        out_shape=tuple(jax.ShapeDtypeStruct(shape, jnp.float32) for shape in shapes),
        in_specs=[VMEM] * len(operands),
        out_specs=(VMEM,) * len(shapes),
        compiler_params=SMALL,
        cost_estimate=SOON,
        name=name,
    )(*operands)


DOT = object()


def finish_kernel(segments, count, *refs):
    out = refs[count]
    for left in range(0, out.shape[1], 128):
        rows_of = []
        for _, _, rows, terms in segments:
            value = None
            for operand, place, first in terms:
                term = refs[operand][place, first : first + rows, left : left + 128]
                value = term if value is None else value + term
            rows_of.append(value)
        value = jnp.concatenate(rows_of, axis=0) if len(rows_of) > 1 else rows_of[0]
        out[0, left : left + 128, :] = value.T.astype(out.dtype)


def finish(segments, head, width, token):
    if width % 128:
        (value,) = plain_blocks(None, None, width, [segments])
        return value.swapaxes(1, 2).astype(jnp.bfloat16)
    operands = []
    (static,) = number_operands([segments], operands)
    operands.append(token)
    return pl.pallas_call(
        functools.partial(finish_kernel, static, len(operands)),
        out_shape=jax.ShapeDtypeStruct((1, width, head), jnp.bfloat16),
        in_specs=[VMEM] * len(operands),
        out_specs=VMEM,
        compiler_params=SMALL,
        cost_estimate=SOON,
        name="finish",
    )(*operands)


class Section:
    def __init__(self, half, chips):
        self.half = half
        self.dots = [True] * chips
        self.given = [[] for _ in range(chips)]

    def add(self, block, low, high, array, slab=0):
        self.given[block].append((low, high, array, slab, low))

    def settle(self, block, low, high, array, slab=0):
        kept = []
        for first, last, other, place, top in self.given[block]:
            for start, stop in ((first, min(last, low)), (max(first, high), last)):
                if start < stop:
                    kept.append((start, stop, other, place, top))
        self.given[block] = kept
        self.add(block, low, high, array, slab)

    def segments(self, block, low, high, slab=0):
        edges = {low, high}
        for start, stop, *_ in self.given[block]:
            edges |= {start, stop}
        edges = sorted(edge for edge in edges if low <= edge <= high)
        made = []
        for start, stop in zip(edges, edges[1:]):
            terms = [(DOT, self.half, 2 * block, start)] if self.dots[block] else []
            terms += [
                (array, place, start - top)
                for first, last, array, place, top in self.given[block]
                if first <= start and stop <= last
            ]
            made.append((slab, start - low, stop - start, terms))
        return made


def order(chips, head):
    last = chips - 1
    half = head // 2
    everything = list(reversed(range(chips)))
    pairs = [(1, block) for block in everything[1:]] + [(0, block) for block in everything]
    if chips < 4:
        events = [("core", *pairs)]
        events += [("up", (block, 0, head)) for block in everything] + [("base", *everything)]
        return events + [("down", (block, 0, head)) for block in everything[:-1]]
    events = [
        ("core", *pairs),
        ("up", (last, 0, half)),
        ("raw upper", last, half, head),
        ("up", (last - 1, 0, half), (1, 0, half)),
        ("base", *everything),
        ("down", (last, 0, half)),
        ("raw lower", last, half, head),
        ("up", (last - 1, half, head), (1, half, head)),
    ]
    for block in reversed(range(2, last - 1)):
        events += [("up", (block, 0, head)), ("down", (block + 1, 0, head))]
    parts = [(0, half), (half, head)] if last - 1 == 2 else [(0, head)]
    events += [("down", (1, 0, half)), ("down", (2, *parts[0])), ("up", (0, 0, head))]
    events += [("down", (2, *part)) for part in parts[1:]]
    return events + [("down", (1, half, head))]


def body(activations, queries, keys, grad_out, segment_ids):
    ways = lax.axis_size("dp")
    slots = lax.axis_size("pipe")
    chips = ways // 2
    head = queries.shape[3]
    width = activations.shape[3] // ways
    last = chips - 1

    def swap(block, distance):
        return lax.ppermute(block, "dp", [(i, i ^ distance) for i in range(ways)])

    def mirror(block):
        return lax.ppermute(block, "pipe", [(i, slots - 1 - i) for i in range(slots)])

    grads, first = front(
        activations, queries, keys, grad_out, segment_ids, 2 * last + 1, width
    )
    lower, upper = Section(0, chips), Section(1, chips)
    upper.add(last, 0, head, swap(first, 1))
    token = None

    def make(name, plan):
        nonlocal token
        *made, token = blocks(name, activations, grads, width, plan, token)
        return made

    def exchange(wanted):
        plan = [
            (slab, 0, head, [(DOT, section.half, 2 * block + 1, 0)])
            for slab, (section, block) in enumerate(wanted)
        ]
        got = swap(make("theirs", [plan])[0], 1)
        for slab, (section, block) in enumerate(wanted):
            section.add(block, 0, head, got, slab)

    def send_up(*wanted):
        plan = []
        for slab, rows in enumerate(wanted):
            plan += upper.segments(*rows, slab)
        (part,) = make("upper", [plan])
        got = mirror(part)
        for slab, rows in enumerate(wanted):
            late.append((*rows, got, slab))

    def send_raw(name, block, low, high):
        bit = block & -block
        sections = {"raw": (upper, lower), "raw upper": (upper,), "raw lower": (lower,)}[name]
        plan = []
        for slab, section in enumerate(sections):
            plan += section.segments(block, low, high, slab)
        got = swap(make("raw", [plan])[0], 2 * bit)
        for slab, section in enumerate(sections):
            if section is upper:
                upper.add(block ^ bit, low, high, got, slab)
            else:
                late.append((block ^ bit, low, high, got, slab))

    def send_down(*wanted):
        bit = wanted[0][0] & -wanted[0][0]
        plan = []
        for slab, rows in enumerate(wanted):
            arrive(*rows)
            plan += lower.segments(*rows, slab)
        (part,) = make("lower", [plan])
        got = swap(part, 2 * bit)
        for slab, (block, low, high) in enumerate(wanted):
            late.append((block ^ bit, low, high, got, slab))

    def settle(blocks_of):
        sums = make("base", [lower.segments(block, 0, head) for block in blocks_of])
        for block, array in zip(blocks_of, sums):
            lower.dots[block] = False
            lower.settle(block, 0, head, array)

    late = []

    def arrive(block, low, high):
        waiting = late[:]
        late.clear()
        for entry in waiting:
            if entry[0] == block and low <= entry[1] and entry[2] <= high:
                lower.add(*entry)
            else:
                late.append(entry)

    for event, *what in order(chips, head):
        if event == "core":
            exchange([(upper if half else lower, block) for half, block in what])
        elif event == "base":
            settle(what)
        elif event == "up":
            send_up(*what)
        elif event.startswith("raw"):
            send_raw(event, *what)
        elif event == "down":
            send_down(*what)
    arrive(0, 0, head)
    assert not late
    return finish(lower.segments(0, 0, head), head, width, token)


def solution(mesh):
    spec = P(None, "pipe", "dp", None)
    return jax.shard_map(
        body,
        mesh=mesh,
        in_specs=(spec,) * 5,
        out_specs=P("pipe", "dp", None),
        check_vma=False,
    )
```
